256 devices in a mesh: ctx: 32 (over z, x), dp: 8 (over y, core).
Axes of the slice: x: 4, y: 4, z: 8, core: 2. Of those that a mesh axis runs over, the one named last changes fastest.
Arguments:
- mel_frames: bfloat16 [8, 4096, 128], P('dp', 'ctx'), may hold values from -6 to 6
- conv_weight: bfloat16 [384, 1280], replicated, may hold values from -0.3125 to 0.3125
- conv_bias: float32 [1280], replicated, may hold values from -3 to 3
- video_hidden: bfloat16 [8, 4096, 5120], P('dp', 'ctx'), may hold values from -6 to 6
- video_count: int32 [8, 32], P('dp', 'ctx'), may hold values from 0 to 128, as said below
- video_places: int32 [8, 4096], P('dp', 'ctx'), may hold values from 0 to 6143, as said below
- audio_places: int32 [8, 4096], P('dp', 'ctx'), may hold values from 0 to 6143, as said below
- cotangent: bfloat16 [8, 6144, 3584], P('dp', 'ctx'), may hold values from -0.049804688 to 0.049804688
Outputs:
- grad_merger: float32 [32, 640, 896], P('ctx', 'dp')
- grad_audio: float32 [32, 160, 896], P('ctx', 'dp')
The draws below stay inside these ranges and needn't reach their ends.
Inputs may be any that keep to these rules, and one draw needn't show every extreme that they name: `video_count`: in every sequence, shards 2i and 2i + 1 of encoder time hold 128 live video rows together, and some shard holds 128. `video_places`: in each sequence the live video slots (slot index within its shard below the shard's count) and the audio rows name every position exactly once; slots at or past the count hold arbitrary positions. `audio_places`: see video_places.
All inputs are finite; a program needn't handle non-finite values.
Results may differ from the reference program's by a relative error of at most 0.0029.
Values may be sent and summed in bfloat16 or wider, within the bound.
A program may use at most 128 MiB of HBM per device.

```python
import jax
import jax.numpy as jnp
from jax import lax

MELS = 128
ENC = 1280
HID = 5120
OUT = 3584
AUD_DEV = 128
VID_MEAN = 64
GRID_ROWS = 8
VID_CAP = 128
SEQ_DEV = 192
SEQ = 6144
MEL = 4096
VID_SLOTS = 4096
N_CTX = 32
N_DP = 8


def layout_draw(key):
    base = jax.random.fold_in(key, 4242)
    key_first, key_which, key_flip, key_junk = jax.random.split(base, 4)
    half_count = N_CTX // 2
    first = jax.random.randint(key_first, (N_DP, half_count), 0, 2 * VID_MEAN + 1)
    which = jax.random.randint(key_which, (N_DP, 1), 0, half_count)
    flipped = jax.random.randint(key_flip, (N_DP, 1), 0, 2)
    first = jnp.where(jnp.arange(half_count)[None, :] == which, flipped * (2 * VID_MEAN), first)
    counts = jnp.stack([first, 2 * VID_MEAN - first], axis=2).reshape(N_DP, N_CTX).astype(jnp.int32)
    shard_sizes = counts + AUD_DEV
    offsets = jnp.cumsum(shard_sizes, axis=1) - shard_sizes
    quarter = AUD_DEV // 4
    slot_ids = jnp.arange(VID_CAP, dtype=jnp.int32)[None, None, :]
    live_rows = counts[:, :, None]
    span_ids = jnp.minimum(4 * slot_ids // jnp.maximum(live_rows, 1), 3)
    video_spots = offsets[:, :, None] + slot_ids + span_ids * quarter
    junk = jax.random.randint(key_junk, (N_DP, N_CTX, VID_CAP), 0, SEQ_DEV * N_CTX)
    video_spots = jnp.where(slot_ids < live_rows, video_spots, junk).reshape(N_DP, N_CTX * VID_CAP)
    row_ids = jnp.arange(AUD_DEV, dtype=jnp.int32)[None, None, :]
    audio_spans = row_ids // quarter
    audio_spots = offsets[:, :, None] + ((audio_spans + 1) * live_rows + 3) // 4 + row_ids
    audio_spots = audio_spots.reshape(N_DP, N_CTX * AUD_DEV)
    return (counts, video_spots.astype(jnp.int32), audio_spots.astype(jnp.int32))


def draw_video_count(key, part):
    return layout_draw(key)[0]


def draw_video_places(key, part):
    return layout_draw(key)[1]


def draw_audio_places(key, part):
    return layout_draw(key)[2]


def block_levels(own_key, shape, shards, low, top_value):
    gain, own = 1.0, jax.random.fold_in(own_key, 6)
    for dim, blocks in shards:
        heights = jnp.exp(jax.random.uniform(jax.random.fold_in(own, dim), (blocks,), jnp.float32, low / len(shards), top_value / len(shards)))
        gain = gain * jnp.repeat(heights, shape[dim] // blocks).reshape([-1 if axis == dim else 1 for axis in range(len(shape))])
    return gain


def centred(rng, extent, scale, most, pieces=(), kind=jnp.bfloat16):
    array = scale * jax.random.normal(rng, extent, jnp.float32)
    if pieces:
        array = array * block_levels(rng, extent, pieces, -0.22, 0.18)
    return jnp.clip(array, -most, most).astype(kind)


def setup_inputs(seed: int = 0) -> dict:
    keys = jax.random.split(jax.random.key(seed), 9)
    return {
        "mel_frames": centred(keys[0], (N_DP, MEL, MELS), 1.0, 6.0, ((0, 8), (1, 32))),
        "conv_weight": centred(keys[1], (3 * MELS, ENC), (3 * MELS) ** -0.5, 0.3125),
        "conv_bias": centred(keys[2], (ENC,), 0.5, 3.0, (), jnp.float32),
        "video_hidden": centred(keys[3], (N_DP, VID_SLOTS, HID), 1.0, 6.0, ((0, 8), (1, 32))),
        "video_count": draw_video_count(jax.random.fold_in(keys[8], 71), 0),
        "video_places": draw_video_places(jax.random.fold_in(keys[8], 71), 0),
        "audio_places": draw_audio_places(jax.random.fold_in(keys[8], 71), 0),
        "cotangent": centred(keys[7], (N_DP, SEQ, OUT), 0.0078125, 0.049804688, ((0, 8), (1, 32))),
    }


def windows_of(frames):
    zero_frame = jnp.zeros((1, frames.shape[1]), frames.dtype)
    padded = jnp.concatenate([zero_frame, frames, zero_frame], axis=0)
    return jnp.concatenate([padded[:-2], padded[1:-1], padded[2:]], axis=1)


def blocks_of(matrix):
    grid_cols = N_CTX // GRID_ROWS
    row_count = matrix.shape[0] // GRID_ROWS
    col_count = matrix.shape[1] // grid_cols
    shaped = matrix.reshape(GRID_ROWS, row_count, grid_cols, col_count)
    return shaped.transpose(0, 2, 1, 3).reshape(N_CTX, row_count, col_count)


def reference(mel_frames, conv_weight, conv_bias, video_hidden, video_count, video_places, audio_places, cotangent):
    def one_sequence(carry, items):
        frames, hidden, counts, places, audio_spots, upstream = items
        conv_out = jnp.dot(windows_of(frames), conv_weight, preferred_element_type=jnp.float32) + conv_bias
        audio_hidden = jax.nn.gelu(conv_out, approximate=False).astype(jnp.bfloat16)
        slot_ids = jnp.arange(hidden.shape[0], dtype=jnp.int32)
        live = (slot_ids % VID_CAP) < jnp.repeat(counts, VID_CAP, total_repeat_length=hidden.shape[0])
        picked = jnp.take(upstream, jnp.where(live, places, 0).astype(jnp.int32), axis=0)
        picked = jnp.where(live[:, None], picked, jnp.zeros_like(picked))
        merger_grad = jnp.dot(hidden.T, picked, preferred_element_type=jnp.float32)
        audio_picked = jnp.take(upstream, audio_spots.astype(jnp.int32), axis=0)
        audio_grad = jnp.dot(audio_hidden.T, audio_picked, preferred_element_type=jnp.float32)
        return (carry[0] + merger_grad, carry[1] + audio_grad), None

    start = (jnp.zeros((HID, OUT), jnp.float32), jnp.zeros((ENC, OUT), jnp.float32))
    (merger_sum, audio_sum), _ = lax.scan(one_sequence, start, (mel_frames, video_hidden, video_count, video_places, audio_places, cotangent))
    return blocks_of(merger_sum), blocks_of(audio_sum)
```

```python
import jax
import jax.numpy as jnp
from jax import lax
from jax.sharding import Mesh, PartitionSpec as P

GRID_ROWS = 8
GRID_COLS = 4


def local(mel, conv_weight, conv_bias, video_hidden, video_count, video_places, audio_places, cotangent):
    z = lax.axis_index("z")
    hidden = video_hidden[0]
    places = video_places[0]
    upstream = cotangent[0]
    block_cols = upstream.shape[1] // GRID_COLS
    enc = conv_weight.shape[1] // GRID_ROWS

    cols = lax.all_to_all(
        jnp.transpose(upstream.reshape(-1, GRID_COLS, block_cols), (1, 0, 2)), "x", 0, 0, tiled=True
    )
    up = lax.all_gather(cols, "z", tiled=True).reshape(-1, block_cols)

    live_count = video_count[0, 0]
    middle = hidden.shape[0] // 2
    pairs = [(i, i ^ 1) for i in range(lax.axis_size("x"))]
    got_rows, got_places = lax.ppermute((hidden[middle:], places[middle:]), "x", pairs)
    joined = jnp.concatenate([hidden[:middle], got_rows], axis=0)
    joined_places = jnp.concatenate([places[:middle], got_places], axis=0)
    ids = jnp.arange(middle, dtype=jnp.int32)
    source = jnp.where((ids < live_count) | (live_count >= middle), ids, middle + ids - live_count)
    rows = jnp.take(joined, source, axis=0)
    spots = jnp.take(joined_places, source, axis=0)
    rows = lax.all_to_all(
        jnp.transpose(rows.reshape(middle, GRID_ROWS, -1), (1, 0, 2)), "z", 0, 0, tiled=True
    )
    rows = lax.all_gather(rows, "x", axis=1, tiled=False)
    rows = rows.reshape(-1, rows.shape[-1])
    spots = lax.all_gather(lax.all_gather(spots, "x"), "z").reshape(-1)

    frames = lax.all_gather(lax.all_gather(mel[0], "x"), "z").reshape(-1, mel.shape[-1])
    audio_spots = lax.all_gather(lax.all_gather(audio_places[0], "x"), "z").reshape(-1)
    pad = jnp.zeros((1, frames.shape[1]), frames.dtype)
    padded = jnp.concatenate([pad, frames, pad], axis=0)
    windows = jnp.concatenate([padded[:-2], padded[1:-1], padded[2:]], axis=1)
    weight = lax.dynamic_slice_in_dim(conv_weight, z * enc, enc, axis=1)
    bias = lax.dynamic_slice_in_dim(conv_bias, z * enc, enc, axis=0)
    conv = jnp.dot(windows, weight, preferred_element_type=jnp.float32) + bias
    audio = jax.nn.gelu(conv, approximate=False).astype(jnp.bfloat16)

    contract = (((0,), (0,)), ((), ()))
    merger = lax.dot_general(rows, jnp.take(up, spots, axis=0), contract, preferred_element_type=jnp.float32)
    audio_block = lax.dot_general(
        audio, jnp.take(up, audio_spots, axis=0), contract, preferred_element_type=jnp.float32
    )
    merger = lax.psum_scatter(merger, ("y", "core"), tiled=True)
    audio_block = lax.psum_scatter(
        audio_block.reshape(GRID_ROWS, enc // GRID_ROWS, block_cols), ("y", "core"), tiled=True
    )
    return merger[None], audio_block


def solution(mesh):
    whole = Mesh(mesh.devices.reshape(8, 4, 4, 2), ("z", "x", "y", "core"))
    dp, ctx = ("y", "core"), ("z", "x")
    return jax.shard_map(
        local,
        mesh=whole,
        in_specs=(
            P(dp, ctx, None),
            P(),
            P(),
            P(dp, ctx, None),
            P(dp, ctx),
            P(dp, ctx),
            P(dp, ctx),
            P(dp, ctx, None),
        ),
        out_specs=(P(ctx, dp, None), P(ctx, dp, None)),
        check_vma=False,
    )
```

```python
import jax
import jax.numpy as jnp
from jax import lax
from jax.experimental import pallas as pl
from jax.experimental.pallas import tpu as pltpu
from jax.sharding import Mesh, PartitionSpec as P

Z, X, Y, C = 8, 4, 4, 2
MELS, ENC, HID, OUT = 128, 1280, 5120, 3584
FRAMES, SLOTS, SPOTS = 128, 128, 192
BLOCK = OUT // X
WIDE = 512
RROWS = HID // X
ROWS = HID // Z // (Y * C)
AROWS = ENC // Z // (Y * C)
APAD = 24
PART = 2 * ROWS + 2 * APAD
LIVE = 256

bf16, f32, i32 = jnp.bfloat16, jnp.float32, jnp.int32
MESH = pl.DeviceIdType.MESH


def dot(a, b, dims=((1,), (0,))):
    return lax.dot_general(a, b, (dims, ((), ())), preferred_element_type=f32)


def iota(shape, dim):
    return lax.broadcasted_iota(i32, shape, dim)


def one_hot(mask):
    return jnp.where(mask, 1.0, 0.0).astype(bf16)


def kernel(
    mel, convw, bias, hidden, count, vplaces, aplaces, cot,
    out_m, out_a,
    ints, ints_x, ints_all, mel_all, b_all, a_raw, a_all, a_t, windows, conv_t, w_ext,
    spot, picked, merger, audio, aud_send, aud_recv, aud_part, own, core_send, core_recv,
    y_send, y_recv, fin_send, fin_recv, ssem, rsem,
):
    z, x = lax.axis_index("z"), lax.axis_index("x")
    y, core = lax.axis_index("y"), lax.axis_index("core")

    def zmod(v):
        return lax.rem(v + 2 * Z, Z)

    def xmod(v):
        return lax.rem(v + 2 * X, X)

    def ymod(v):
        return lax.rem(v + Y, Y)

    home_x = lax.div(z, 2)
    half = lax.rem(z, 2)

    barrier = pltpu.get_barrier_semaphore()
    peers = [{"z": zmod(z + k)} for k in range(1, Z)]
    peers += [{"x": xmod(x + k)} for k in range(1, X)]
    peers += [{"y": ymod(y + k)} for k in range(1, Y)]
    peers += [{"core": 1 - core}]
    for peer in peers:
        pl.semaphore_signal(barrier, inc=1, device_id=peer, device_id_type=MESH)
    for zl in range(2):
        to_z = 2 * x + zl

        @pl.when(jnp.logical_or(to_z != z, home_x != x))
        def _():
            pl.semaphore_signal(
                barrier, inc=1, device_id={"z": to_z, "x": home_x}, device_id_type=MESH
            )

    pl.semaphore_wait(barrier, len(peers) + 1 + jnp.where(home_x != x, 1, 0))

    sent = []
    names = {}

    def sem(*key):
        return names.setdefault(key, len(names))

    def copy(src, dst, key, device):
        i = sem(*key)
        return pltpu.make_async_remote_copy(
            src_ref=src, dst_ref=dst, send_sem=ssem.at[i], recv_sem=rsem.at[i],
            device_id=device, device_id_type=MESH,
        )

    def send(src, dst, key, device):
        c = copy(src, dst, key, device)
        c.start()
        sent.append(c)

    def arrived(dst, *key):
        copy(dst, dst, key, {"core": 1 - core}).wait_recv()

    def window(zt):
        return pl.ds(pl.multiple_of(lax.div(zt, 2) * BLOCK + lax.rem(zt, 2) * (BLOCK - WIDE), 128), WIDE)

    def b_rows(xs, zs):
        return b_all.at[xs, pl.ds(pl.multiple_of(zs * SPOTS, 64), SPOTS)]

    def a_cols(xt):
        return pl.ds(pl.multiple_of(xt * RROWS, 128), RROWS)

    ints[0:1, :] = aplaces[...]
    ints[1:2, :] = vplaces[...]
    ints[2:3, :] = jnp.broadcast_to(count[...], (1, 128))
    ints[3:8, :] = jnp.zeros((5, 128), i32)
    ints_x[x] = ints[...]
    ints_all[x, z] = ints[...]
    mel_all[x, z] = mel[...]

    for k in range(1, X):
        xt = xmod(x + k)
        send(ints, ints_x.at[x], ("ix", k), {"x": xt})
        send(hidden.at[:, a_cols(xt)], a_raw.at[x], ("a", k), {"x": xt})
    own_a = pltpu.make_async_copy(hidden.at[:, a_cols(x)], a_raw.at[x], ssem.at[sem("own_a")])
    own_a.start()
    own_b = pltpu.make_async_copy(cot.at[:, window(z)], b_rows(x, z), ssem.at[sem("own_b")])
    own_b.start()
    for k in range(1, Z):
        zt = zmod(z + k)
        send(ints, ints_all.at[x, z], ("iz", k), {"z": zt})
        send(mel, mel_all.at[x, z], ("mz", k), {"z": zt})
    for k in (1, 7, 2, 6, 3, 5, 4):
        zt = zmod(z + k)
        send(cot.at[:, window(zt)], b_rows(x, z), ("b", k), {"z": zt})

    right, left = {"x": xmod(x + 1)}, {"x": xmod(x - 1)}

    def b_out(k):
        block = b_rows(x, zmod(z - k))
        send(block, block, ("br", k), right)
        send(block, block, ("bl", k), left)

    own_b.wait()
    b_out(0)

    own_a.wait()
    for k in range(1, X):
        arrived(ints_x.at[xmod(x - k)], "ix", k)
        arrived(a_raw.at[xmod(x - k)], "a", k)

    def selection(held):
        row, col = iota((128, 256), 0), iota((128, 256), 1)
        return one_hot(jnp.where(row < held, row, row - held + 128) == col)

    for j in range(2):
        held = jnp.broadcast_to(ints_x[2 * j, 2:3, :][:, 0:1], (128, 256))
        pair = jnp.concatenate([a_raw[2 * j], a_raw[2 * j + 1]], axis=0)
        a_all[z, j * 128 : (j + 1) * 128, :] = dot(selection(held), pair).astype(bf16)

    up, down = {"z": zmod(z + 1)}, {"z": zmod(z - 1)}
    up_items = [(0, 0), (0, 1), (1, 0), (1, 1), (2, 0), (2, 1), (3, 0)]
    down_items = [(0, 0), (0, 1), (1, 0), (1, 1), (2, 0), (2, 1), (3, 1)]

    def a_rows(zs, j):
        return a_all.at[zs, pl.ds(j * 128, 128)]

    def ring(n):
        for items, name, step, device in ((up_items, "up", -1, up), (down_items, "down", 1, down)):
            t, j = items[n]
            rows = a_rows(zmod(z + step * t), j)
            if t:
                arrived(rows, name, t - 1, j)
            send(rows, rows, (name, t, j), device)

    ring(0)
    ring(1)

    for k in range(1, Z):
        arrived(ints_all.at[x, zmod(z - k)], "iz", k)
        arrived(mel_all.at[x, zmod(z - k)], "mz", k)
    for k in range(1, X):
        xt = xmod(x + k)
        send(ints_all.at[x], ints_all.at[x], ("ixa", k), {"x": xt})
        send(mel_all.at[x], mel_all.at[x], ("mxa", k), {"x": xt})

    b0 = bias[...]
    hi = b0.astype(bf16).astype(f32)
    mid = (b0 - hi).astype(bf16).astype(f32)
    low = b0 - hi - mid
    row = iota((128, ENC), 0)
    w_ext[...] = jnp.where(row == 0, hi, jnp.where(row == 1, mid, jnp.where(row == 2, low, 0.0))).astype(bf16)
    conv_t[:, 0 : 3 * MELS] = convw[...].T
    conv_t[:, 3 * MELS :] = w_ext[...].T

    for k in (1, 7, 2, 6, 3, 5, 4):
        arrived(b_rows(x, zmod(z - k)), "b", k)
        b_out(k)

    for k in range(1, X):
        xs = xmod(x - k)
        arrived(ints_all.at[xs], "ixa", k)
        arrived(mel_all.at[xs], "mxa", k)

    windows[:, 3 * MELS :] = jnp.ones((X * Z * FRAMES, 128), bf16)
    edge = iota((FRAMES, MELS), 0)

    @pl.loop(0, Z)
    def _(zs):
        for xs in range(X):
            own_frames = mel_all[xs, zs].astype(f32)
            zp = zs if xs else jnp.maximum(zs - 1, 0)
            zn = zs if xs < X - 1 else jnp.minimum(zs + 1, Z - 1)
            before = mel_all[(xs - 1) % X, zp].astype(f32)
            after = mel_all[(xs + 1) % X, zn].astype(f32)
            if xs == 0:
                before = jnp.where(jnp.broadcast_to(zs, before.shape) == 0, 0.0, before)
            if xs == X - 1:
                after = jnp.where(jnp.broadcast_to(zs, after.shape) == Z - 1, 0.0, after)
            before = jnp.where(edge == 0, pltpu.roll(before, 1, 0), pltpu.roll(own_frames, 1, 0))
            after = jnp.where(
                edge == FRAMES - 1, pltpu.roll(after, FRAMES - 1, 0), pltpu.roll(own_frames, FRAMES - 1, 0)
            )
            at = pl.ds(pl.multiple_of((xs * Z + zs) * FRAMES, FRAMES), FRAMES)
            windows[at, 0:MELS] = before.astype(bf16)
            windows[at, MELS : 2 * MELS] = own_frames.astype(bf16)
            windows[at, 2 * MELS : 3 * MELS] = after.astype(bf16)

    @pl.loop(0, Z)
    def _(zs):
        for j in range(2):
            held = jnp.broadcast_to(ints_all[2 * j, zs, 2:3, :][:, 0:1], (128, 256))
            pick = selection(held)
            places = jnp.concatenate([ints_all[2 * j, zs, 1:2, :], ints_all[2 * j + 1, zs, 1:2, :]], axis=1)
            high = lax.shift_right_logical(places, 7)
            rest = jnp.bitwise_and(places, 127)
            high = jnp.broadcast_to(high.astype(f32), (128, 256)).astype(bf16)
            rest = jnp.broadcast_to(rest.astype(f32), (128, 256)).astype(bf16)
            value = 128.0 * dot(pick, high, ((1,), (1,))) + dot(pick, rest, ((1,), (1,)))
            spot[pl.ds(pl.multiple_of(zs * LIVE + j * 128, 128), 128), :] = value.astype(i32)

    ring(2)

    audio[...] = jnp.zeros_like(audio)

    def audio_piece(h):
        wpos = []
        for zs in (2 * h, 2 * h + 1):
            base = (zs * X + x) * SPOTS
            here = iota((SPOTS, 128), 0) + base
            total = jnp.zeros((SPOTS, 4 * MELS), f32)

            def shard(xs, total):
                hot = jnp.concatenate(
                    [
                        one_hot(jnp.broadcast_to(ints_all[xs, zt, 0:1, :], (SPOTS, 128)) == here)
                        for zt in range(Z)
                    ],
                    axis=1,
                )
                at = pl.ds(pl.multiple_of(xs * (Z * FRAMES), FRAMES), Z * FRAMES)
                return total + dot(hot, windows[at, :])

            wpos.append(lax.fori_loop(0, X, shard, total).astype(bf16))
        wpos = jnp.concatenate(wpos, axis=0)
        bs = b_all[x, h * 2 * SPOTS : (h + 1) * 2 * SPOTS, :]

        @pl.loop(0, ENC // 256)
        def _(m):
            at = pl.ds(pl.multiple_of(m * 256, 256), 256)
            conv = dot(conv_t[at, :], wpos, ((1,), (1,)))
            act = (0.5 * conv * (1.0 + lax.erf(conv * 0.7071067811865476))).astype(bf16)
            audio[at, :] += dot(act, bs)

    def forward(ks):
        for k in ks:
            zs = zmod(z - k)
            block = b_rows(xmod(x - 1), zs)
            arrived(block, "br", k)
            if k < 4:
                send(block, block, ("fr", k), right)
            block = b_rows(xmod(x + 1), zs)
            arrived(block, "bl", k)
            if k >= 4:
                send(block, block, ("fl", k), left)

    audio_piece(0)
    ring(3)
    forward((0, 1, 7))
    audio_piece(1)
    ring(4)
    forward((2, 6))
    audio_piece(2)
    ring(5)
    forward((3, 5, 4))
    audio_piece(3)
    ring(6)

    for k in range(1, X):
        xt = xmod(x + k)
        aud_send[k] = audio[pl.ds(pl.multiple_of(xt * (ENC // X), 64), ENC // X), :].astype(bf16)
        send(aud_send.at[k], aud_recv.at[k], ("aud", k), {"x": xt})

    lane = iota((256, 128), 1)

    def pick_rows(xs, part, first):
        span = 4 * SPOTS

        @pl.loop(0, Z)
        def _(q):
            at = pl.ds(pl.multiple_of(q * LIVE, LIVE), LIVE)
            spots = spot[at, :]
            tiles = []
            for t in range(span // 128):
                ends = []
                for s in (2 * t, 2 * t + 1):
                    ends.append((4 * part + s // 3) * X * SPOTS + (s % 3) * 64)
                there = jnp.where(lane < 64, lane + ends[0], lane - 64 + ends[1]) + xs * SPOTS
                tiles.append(one_hot(spots == there))
            got = dot(jnp.concatenate(tiles, axis=1), b_all[xs, part * span : (part + 1) * span, :])
            if first:
                picked[at, :] = got
            else:
                picked[at, :] += got

    pick_rows(x, 0, True)
    pick_rows(x, 1, False)
    pick_rows(xmod(x - 1), 0, False)
    pick_rows(xmod(x - 1), 1, False)
    pick_rows(xmod(x + 1), 0, False)
    pick_rows(xmod(x + 1), 1, False)

    for t in range(3):
        for j in range(2):
            if (t + 1, j) not in up_items:
                arrived(a_rows(zmod(z - t - 1), j), "up", t, j)
            if (t + 1, j) not in down_items:
                arrived(a_rows(zmod(z + t + 1), j), "down", t, j)
    arrived(a_rows(zmod(z + 4), 0), "up", 3, 0)
    arrived(a_rows(zmod(z + 4), 1), "down", 3, 1)

    @pl.loop(0, Z)
    def _(zs):
        for j in range(2):
            a_t[:, pl.ds(pl.multiple_of(zs * LIVE + j * 128, 128), 128)] = a_all[
                zs, j * 128 : (j + 1) * 128, :
            ].T

    for k in range(Z):
        arrived(b_rows(xmod(x + 2), zmod(z - k)), "fr" if k < 4 else "fl", k)
    pick_rows(xmod(x + 2), 0, False)
    pick_rows(xmod(x + 2), 1, False)

    total = audio[pl.ds(pl.multiple_of(x * (ENC // X), 64), ENC // X), :]
    for k in range(1, X):
        arrived(aud_recv.at[k], "aud", k)
        total = total + aud_recv[k].astype(f32)
    audio[0 : ENC // X, :] = total
    aud_part[...] = jnp.zeros_like(aud_part)
    for zl in range(2):
        for d in range(Y * C):
            at = (zl * Y * C + d) * AROWS
            aud_part[d, zl * APAD : zl * APAD + AROWS, :] = audio[at : at + AROWS, :]

    @pl.loop(0, RROWS // 256)
    def _(m):
        at = pl.ds(pl.multiple_of(m * 256, 256), 256)
        merger[at, :] = dot(a_t[at, :], picked[...].astype(bf16))

    def merger_rows(zl, d):
        return merger[pl.ds(pl.multiple_of((zl * Y * C + d) * ROWS, 16), ROWS), :]

    other = 1 - core
    for yt in range(Y):
        for zl in range(2):
            core_send[yt, zl * ROWS : (zl + 1) * ROWS, :] = merger_rows(zl, 2 * yt + other).astype(bf16)
            own[yt, zl * ROWS : (zl + 1) * ROWS, :] = merger_rows(zl, 2 * yt + core)
        core_send[yt, 2 * ROWS :, :] = aud_part[2 * yt + other].astype(bf16)
        own[yt, 2 * ROWS :, :] = aud_part[2 * yt + core]
    send(core_send, core_recv, ("core",), {"core": other})
    arrived(core_recv, "core")
    for k in range(1, Y):
        yt = ymod(y + k)
        y_send[k] = (own[yt] + core_recv[yt].astype(f32)).astype(bf16)
        send(y_send.at[k], y_recv.at[k], ("y", k), {"y": yt})
    total = own[y] + core_recv[y].astype(f32)
    for k in range(1, Y):
        arrived(y_recv.at[k], "y", k)
        total = total + y_recv[k].astype(f32)
    for zl in range(2):
        fin_send[zl, 0:ROWS, :] = total[zl * ROWS : (zl + 1) * ROWS]
        fin_send[zl, ROWS:, :] = total[2 * ROWS + zl * APAD : 2 * ROWS + (zl + 1) * APAD]

    fin = sem("fin", 0), sem("fin", 1)
    fin_out = sem("fout", 0), sem("fout", 1)
    for zl in range(2):
        to_z = 2 * x + zl
        elsewhere = jnp.logical_or(to_z != z, home_x != x)
        out = pltpu.make_async_remote_copy(
            src_ref=fin_send.at[zl], dst_ref=fin_recv.at[half], send_sem=ssem.at[fin_out[zl]],
            recv_sem=rsem.at[fin[0] + half], device_id={"z": to_z, "x": home_x}, device_id_type=MESH,
        )

        @pl.when(elsewhere)
        def _():
            out.start()

        @pl.when(jnp.logical_not(elsewhere))
        def _():
            fin_recv[half] = fin_send[zl]

    for h in range(2):
        @pl.when(jnp.logical_or(2 * x + h != z, home_x != x))
        def _():
            arrived(fin_recv.at[h], "fin", h)

    out_m[:, 0:WIDE] = fin_recv[0, 0:ROWS, :]
    out_m[:, WIDE:] = fin_recv[1, 0:ROWS, 2 * WIDE - BLOCK :]
    out_a[:, 0:WIDE] = fin_recv[0, ROWS : ROWS + AROWS, :]
    out_a[:, WIDE:] = fin_recv[1, ROWS : ROWS + AROWS, 2 * WIDE - BLOCK :]

    for c in sent:
        c.wait_send()
    for zl in range(2):
        to_z = 2 * x + zl

        @pl.when(jnp.logical_or(to_z != z, home_x != x))
        def _():
            pltpu.make_async_remote_copy(
                src_ref=fin_send.at[zl], dst_ref=fin_recv.at[half], send_sem=ssem.at[fin_out[zl]],
                recv_sem=rsem.at[fin[0] + half], device_id={"z": to_z, "x": home_x}, device_id_type=MESH,
            ).wait_send()

    assert len(names) <= 128


def local(mel, conv_weight, conv_bias, video_hidden, video_count, video_places, audio_places, cotangent):
    vmem = pl.BlockSpec(memory_space=pltpu.VMEM)
    hbm = pl.BlockSpec(memory_space=pl.ANY)
    part = (PART, WIDE)
    merger, audio = pl.pallas_call(
        kernel,
        out_shape=(
            jax.ShapeDtypeStruct((ROWS, BLOCK), f32),
            jax.ShapeDtypeStruct((AROWS, BLOCK), f32),
        ),
        in_specs=[vmem, vmem, vmem, hbm, vmem, vmem, vmem, hbm],
        out_specs=(vmem, vmem),
        scratch_shapes=[
            pltpu.VMEM((8, 128), i32),
            pltpu.VMEM((X, 8, 128), i32),
            pltpu.VMEM((X, Z, 8, 128), i32),
            pltpu.VMEM((X, Z, FRAMES, MELS), bf16),
            pltpu.VMEM((X, Z * SPOTS, WIDE), bf16),
            pltpu.VMEM((X, SLOTS, RROWS), bf16),
            pltpu.VMEM((Z, LIVE, RROWS), bf16),
            pltpu.VMEM((RROWS, Z * LIVE), bf16),
            pltpu.VMEM((X * Z * FRAMES, 4 * MELS), bf16),
            pltpu.VMEM((ENC, 4 * MELS), bf16),
            pltpu.VMEM((128, ENC), bf16),
            pltpu.VMEM((Z * LIVE, 128), i32),
            pltpu.VMEM((Z * LIVE, WIDE), f32),
            pltpu.VMEM((RROWS, WIDE), f32),
            pltpu.VMEM((ENC, WIDE), f32),
            pltpu.VMEM((X, ENC // X, WIDE), bf16),
            pltpu.VMEM((X, ENC // X, WIDE), bf16),
            pltpu.VMEM((Y * C, 2 * APAD, WIDE), f32),
            pltpu.VMEM((Y, *part), f32),
            pltpu.VMEM((Y, *part), bf16),
            pltpu.VMEM((Y, *part), bf16),
            pltpu.VMEM((Y, *part), bf16),
            pltpu.VMEM((Y, *part), bf16),
            pltpu.VMEM((2, ROWS + APAD, WIDE), f32),
            pltpu.VMEM((2, ROWS + APAD, WIDE), f32),
            pltpu.SemaphoreType.DMA((128,)),
            pltpu.SemaphoreType.DMA((128,)),
        ],
        compiler_params=pltpu.CompilerParams(
            collective_id=0, has_side_effects=True, vmem_limit_bytes=60 * 2**20
        ),
    )(
        mel[0], conv_weight, conv_bias[None], video_hidden[0],
        video_count, video_places, audio_places, cotangent[0],
    )
    return merger[None], audio[None]


def solution(mesh):
    whole = Mesh(mesh.devices.reshape(Z, X, Y, C), ("z", "x", "y", "core"))
    dp, ctx = ("y", "core"), ("z", "x")
    return jax.shard_map(
        local,
        mesh=whole,
        in_specs=(
            P(dp, ctx, None),
            P(),
            P(),
            P(dp, ctx, None),
            P(dp, ctx),
            P(dp, ctx),
            P(dp, ctx),
            P(dp, ctx, None),
        ),
        out_specs=(P(ctx, dp, None), P(ctx, dp, None)),
        check_vma=False,
    )
```

```python
import jax
import jax.numpy as jnp
from jax import lax
from jax.experimental import pallas as pl
from jax.experimental.pallas import tpu as pltpu
from jax.sharding import Mesh, PartitionSpec as P

Z, X, Y, C = 8, 4, 4, 2
MELS, ENC, HID, OUT = 128, 1280, 5120, 3584
FRAMES, SLOTS, SPOTS = 128, 128, 192
BLOCK = OUT // X
WIDE = 512
RROWS = HID // X
ROWS = HID // Z // (Y * C)
AROWS = ENC // Z // (Y * C)
APAD = 32
PART = ROWS + APAD
KEEP = 24
HALF = 256
EROWS = ENC // Z
ZROWS = HID // Z
LIVE = 256

bf16, f32, i32 = jnp.bfloat16, jnp.float32, jnp.int32
MESH = pl.DeviceIdType.MESH


def dot(a, b, dims=((1,), (0,))):
    return lax.dot_general(a, b, (dims, ((), ())), preferred_element_type=f32)


def iota(shape, dim):
    return lax.broadcasted_iota(i32, shape, dim)


def one_hot(mask):
    return jnp.where(mask, 1.0, 0.0).astype(bf16)


def kernel(
    mel, convw, bias, hidden, count, vplaces, aplaces, cot,
    out_m, out_a,
    ints, ints_x, ints_all, mel_all, b_all, a_raw, a_all, a_t, windows, conv_t, w_ext,
    spot, picked, picked_b, merger, acts, audio, aud_send, aud_relay, aud_recv, aud_part, own, core_send, core_recv,
    y_send, y_relay, y_recv, fin_send, fin_recv, fina_send, fina_recv, a_relay, b_relay, ssem, rsem,
):
    z, x = lax.axis_index("z"), lax.axis_index("x")
    y, core = lax.axis_index("y"), lax.axis_index("core")

    def zmod(v):
        return lax.rem(v + 2 * Z, Z)

    def xmod(v):
        return lax.rem(v + 2 * X, X)

    def ymod(v):
        return lax.rem(v + Y, Y)

    home_x = lax.div(z, 2)
    half = lax.rem(z, 2)

    barrier = pltpu.get_barrier_semaphore()
    peers = [{"z": zmod(z + k)} for k in range(1, Z)]
    peers += [{"x": xmod(x + k)} for k in range(1, X)]
    peers += [{"y": ymod(y + k)} for k in range(1, Y)]
    peers += [{"core": 1 - core}]
    for peer in peers:
        pl.semaphore_signal(barrier, inc=1, device_id=peer, device_id_type=MESH)
    for h in range(2):

        @pl.when(jnp.logical_or(2 * x + h != z, lax.rem(z, X) != x))
        def _():
            pl.semaphore_signal(
                barrier, inc=1, device_id={"z": 2 * x + h, "x": lax.rem(z, X)}, device_id_type=MESH
            )

    here = jnp.logical_and(home_x == x, lax.rem(z, X) == x)
    pl.semaphore_wait(barrier, len(peers) + 2 - jnp.where(here, 1, 0))

    sent = []
    names = {}

    def sem(*key):
        return names.setdefault(key, len(names))

    def copy(src, dst, key, device):
        i = sem(*key)
        return pltpu.make_async_remote_copy(
            src_ref=src, dst_ref=dst, send_sem=ssem.at[i], recv_sem=rsem.at[i],
            device_id=device, device_id_type=MESH,
        )

    def send(src, dst, key, device):
        c = copy(src, dst, key, device)
        c.start()
        sent.append(c)

    def arrived(dst, *key):
        copy(dst, dst, key, {"core": 1 - core}).wait_recv()

    def window(zt):
        return pl.ds(pl.multiple_of(lax.div(zt, 2) * BLOCK + lax.rem(zt, 2) * (BLOCK - WIDE), 128), WIDE)

    def b_rows(xs, zs):
        return b_all.at[xs, pl.ds(pl.multiple_of(zs * SPOTS, 64), SPOTS)]

    def b_half(zs, h):
        return b_all.at[x, pl.ds(pl.multiple_of(zs * SPOTS + h * 96, 32), 96)]

    def a_cols(xt, w):
        return hidden.at[:, pl.ds(pl.multiple_of((xt + X * w) * ZROWS, 128), ZROWS)]

    def a_slot(xs, w):
        return a_raw.at[xs, :, pl.ds(w * ZROWS, ZROWS)]

    right, left = {"x": xmod(x + 1)}, {"x": xmod(x - 1)}
    sides = ((1, right), (-1, left))

    ints[0:1, :] = aplaces[...]
    ints[1:2, :] = vplaces[...]
    ints[2:3, :] = jnp.broadcast_to(count[...], (1, 128))
    ints[3:8, :] = jnp.zeros((5, 128), i32)
    ints_x[x] = ints[...]
    ints_all[x, z] = ints[...]
    mel_all[x, z] = mel[...]

    for k in range(1, Z):
        zt = zmod(z + k)
        send(ints, ints_all.at[x, z], ("iz", k), {"z": zt})
        send(mel, mel_all.at[x, z], ("mz", k), {"z": zt})
    for k in range(1, X):
        send(ints, ints_x.at[x], ("ix", k), {"x": xmod(x + k)})
    for w, (step, side) in enumerate(sides):
        send(a_cols(xmod(x + 2), w), a_relay.at[w], ("a2", w), side)
    for step, side in sides:
        for w in range(2):
            send(a_cols(xmod(x + step), w), a_slot(x, w), ("a", step, w), side)
    own_a = []
    for w in range(2):
        c = pltpu.make_async_copy(a_cols(x, w), a_slot(x, w), ssem.at[sem("own_a", w)])
        c.start()
        own_a.append(c)
    own_b = pltpu.make_async_copy(cot.at[:, window(z)], b_rows(x, z), ssem.at[sem("own_b")])
    own_b.start()
    zt = zmod(z + 4)
    send(cot.at[pl.ds(96, 96), window(zt)], b_relay, ("b4",), {"z": zmod(z - 1)})
    for k in (1, 7, 2, 6, 3, 5):
        zt = zmod(z + k)
        send(cot.at[:, window(zt)], b_rows(x, z), ("b", k), {"z": zt})
    zt = zmod(z + 4)
    send(cot.at[pl.ds(0, 96), window(zt)], b_half(z, 0), ("b", 4), {"z": zt})

    def b_out(k):
        block = b_rows(x, zmod(z - k))
        send(block, block, ("br", k), right)
        send(block, block, ("bl", k), left)


    def selection(held):
        row, col = iota((128, 256), 0), iota((128, 256), 1)
        return one_hot(jnp.where(row < held, row, row - held + 128) == col)

    up, down = {"z": zmod(z + 1)}, {"z": zmod(z - 1)}
    up_items = [(0, 0), (0, 1), (1, 0), (1, 1), (2, 0), (2, 1), (3, 0)]
    down_items = [(0, 0), (0, 1), (1, 0), (1, 1), (2, 0), (2, 1), (3, 1)]

    def pair(j):
        return lax.rem(lax.div(x, 2) + j, 2)

    def a_rows(zs, j):
        return a_all.at[zs, pl.ds(pl.multiple_of(pair(j) * 128, 128), 128)]

    def pack(j):
        p = pair(j)
        held = jnp.broadcast_to(ints_x[2 * p, 2:3, :][:, 0:1], (128, 256))
        both = jnp.concatenate([a_raw[2 * p], a_raw[2 * p + 1]], axis=0)
        a_all[z, pl.ds(pl.multiple_of(p * 128, 128), 128), :] = dot(selection(held), both).astype(bf16)

    def ring(n):
        for items, name, step, device in ((up_items, "up", -1, up), (down_items, "down", 1, down)):
            t, j = items[n]
            rows = a_rows(zmod(z + step * t), j)
            if t:
                arrived(rows, name, t - 1, j)
            send(rows, rows, (name, t, j), device)

    for w, (step, side) in enumerate(sides):
        arrived(a_relay.at[w], "a2", w)
        send(a_relay.at[w], a_slot(xmod(x - step), w), ("a3", w), side)
    own_b.wait()
    b_out(0)

    b0 = bias[...]
    hi = b0.astype(bf16).astype(f32)
    mid = (b0 - hi).astype(bf16).astype(f32)
    low = b0 - hi - mid
    row = iota((128, ENC), 0)
    w_ext[...] = jnp.where(row == 0, hi, jnp.where(row == 1, mid, jnp.where(row == 2, low, 0.0))).astype(bf16)
    conv_t[:, 0 : 3 * MELS] = convw[...].T
    conv_t[:, 3 * MELS :] = w_ext[...].T

    for k in range(1, Z):
        arrived(ints_all.at[x, zmod(z - k)], "iz", k)
        arrived(mel_all.at[x, zmod(z - k)], "mz", k)
    def mel_half(xs, w):
        return mel_all.at[xs, pl.ds(w * (Z // 2), Z // 2)]

    for k in range(1, X):
        send(ints_all.at[x], ints_all.at[x], ("ixa", k), {"x": xmod(x + k)})
    for w in range(2):
        for step, side in sides:
            send(mel_half(x, w), mel_half(x, w), ("mxa", step, w), side)

    for c in own_a:
        c.wait()
    for k in range(1, X):
        arrived(ints_x.at[xmod(x - k)], "ix", k)
    for w, (step, side) in enumerate(sides):
        for v in range(2):
            arrived(a_slot(xmod(x - step), v), "a", step, v)
    pack(0)
    ring(0)
    for w in range(2):
        arrived(a_slot(xmod(x + 2), w), "a3", w)
    pack(1)
    ring(1)

    def forward(ks):
        for k in ks:
            zs = zmod(z - k)
            block = b_rows(xmod(x - 1), zs)
            arrived(block, "br", k)
            if k < 4:
                send(block, block, ("fr", k), right)
            block = b_rows(xmod(x + 1), zs)
            arrived(block, "bl", k)
            if k >= 4:
                send(block, block, ("fl", k), left)

    def audio_piece(h):
        wpos = []
        for zs in (2 * h, 2 * h + 1):
            base = (zs * X + x) * SPOTS
            here = iota((SPOTS, 128), 0) + base
            total = jnp.zeros((SPOTS, 4 * MELS), f32)

            def shard(xs, total):
                hot = jnp.concatenate(
                    [
                        one_hot(jnp.broadcast_to(ints_all[xs, zt, 0:1, :], (SPOTS, 128)) == here)
                        for zt in range(Z)
                    ],
                    axis=1,
                )
                at = pl.ds(pl.multiple_of(xs * (Z * FRAMES), FRAMES), Z * FRAMES)
                return total + dot(hot, windows[at, :])

            wpos.append(lax.fori_loop(0, X, shard, total).astype(bf16))
        wpos = jnp.concatenate(wpos, axis=0)

        @pl.loop(0, ENC // 256)
        def _(m):
            at = pl.ds(pl.multiple_of(m * 256, 256), 256)
            conv = dot(conv_t[at, :], wpos, ((1,), (1,)))
            act = (0.5 * conv * (1.0 + lax.erf(conv * 0.7071067811865476))).astype(bf16)
            acts[at, h * 2 * SPOTS : (h + 1) * 2 * SPOTS] = act

    def b_in(ks):
        for k in ks:
            arrived(b_rows(x, zmod(z - k)), "b", k)
            b_out(k)

    for w, (step, side) in enumerate(sides):
        rows = mel_half(xmod(x - step), w)
        arrived(rows, "mxa", step, w)
        send(rows, rows, ("mxb", w), side)
    arrived(b_relay, "b4")
    send(b_relay, b_half(zmod(z + 1), 1), ("b5",), {"z": zmod(z - 3)})
    for k in (1, 7):
        arrived(b_rows(x, zmod(z - k)), "b", k)
        b_out(k)

    forward((0,))
    for k in range(1, X):
        arrived(ints_all.at[xmod(x - k)], "ixa", k)
    for w, (step, side) in enumerate(sides):
        arrived(mel_half(xmod(x - step), 1 - w), "mxa", step, 1 - w)
        arrived(mel_half(xmod(x + 2), w), "mxb", w)

    windows[:, 3 * MELS :] = jnp.ones((X * Z * FRAMES, 128), bf16)
    edge = iota((FRAMES, MELS), 0)

    @pl.loop(0, Z)
    def _(zs):
        for xs in range(X):
            own_frames = mel_all[xs, zs].astype(f32)
            zp = zs if xs else jnp.maximum(zs - 1, 0)
            zn = zs if xs < X - 1 else jnp.minimum(zs + 1, Z - 1)
            before = mel_all[(xs - 1) % X, zp].astype(f32)
            after = mel_all[(xs + 1) % X, zn].astype(f32)
            if xs == 0:
                before = jnp.where(jnp.broadcast_to(zs, before.shape) == 0, 0.0, before)
            if xs == X - 1:
                after = jnp.where(jnp.broadcast_to(zs, after.shape) == Z - 1, 0.0, after)
            before = jnp.where(edge == 0, pltpu.roll(before, 1, 0), pltpu.roll(own_frames, 1, 0))
            after = jnp.where(
                edge == FRAMES - 1, pltpu.roll(after, FRAMES - 1, 0), pltpu.roll(own_frames, FRAMES - 1, 0)
            )
            at = pl.ds(pl.multiple_of((xs * Z + zs) * FRAMES, FRAMES), FRAMES)
            windows[at, 0:MELS] = before.astype(bf16)
            windows[at, MELS : 2 * MELS] = own_frames.astype(bf16)
            windows[at, 2 * MELS : 3 * MELS] = after.astype(bf16)

    b_in((2, 6))

    @pl.loop(0, Z)
    def _(zs):
        for j in range(2):
            held = jnp.broadcast_to(ints_all[2 * j, zs, 2:3, :][:, 0:1], (128, 256))
            pick = selection(held)
            places = jnp.concatenate([ints_all[2 * j, zs, 1:2, :], ints_all[2 * j + 1, zs, 1:2, :]], axis=1)
            high = lax.shift_right_logical(places, 7)
            rest = jnp.bitwise_and(places, 127)
            high = jnp.broadcast_to(high.astype(f32), (128, 256)).astype(bf16)
            rest = jnp.broadcast_to(rest.astype(f32), (128, 256)).astype(bf16)
            value = 128.0 * dot(pick, high, ((1,), (1,))) + dot(pick, rest, ((1,), (1,)))
            spot[pl.ds(pl.multiple_of(zs * LIVE + j * 128, 128), 128), :] = value.astype(i32)

    ring(2)
    b_in((3, 5))
    forward((1, 7))
    audio_piece(0)
    arrived(b_half(zmod(z - 4), 0), "b", 4)
    arrived(b_half(zmod(z + 4), 1), "b5")
    b_out(4)
    ring(3)
    forward((2, 6))
    audio_piece(1)
    ring(4)
    forward((3, 5))
    audio_piece(2)
    ring(5)
    forward((4,))
    audio_piece(3)

    @pl.loop(0, ENC // 256)
    def _(m):
        at = pl.ds(pl.multiple_of(m * 256, 256), 256)
        audio[at, :] = dot(acts[at, :], b_all[x])

    def audio_rows(xt, w):
        rows = [
            audio[pl.ds(pl.multiple_of((xt + X * zl) * EROWS, 32), EROWS), w * HALF : (w + 1) * HALF]
            for zl in range(2)
        ]
        return jnp.concatenate(rows, axis=0)

    for w, (step, side) in enumerate(sides):
        aud_send[0, w] = audio_rows(xmod(x + 2), w).astype(bf16)
        send(aud_send.at[0, w], aud_relay.at[w], ("aud1", w), side)
        aud_send[1, w] = audio_rows(xmod(x + step), 1 - w).astype(bf16)
        send(aud_send.at[1, w], aud_recv.at[1, w], ("aud2", w), side)

    def audio_relay():
        for w, (step, side) in enumerate(sides):
            arrived(aud_relay.at[w], "aud1", w)
            aud_send[2, w] = (audio_rows(xmod(x + step), w) + aud_relay[w].astype(f32)).astype(bf16)
            send(aud_send.at[2, w], aud_recv.at[0, w], ("aud3", w), side)

    lane = iota((256, 128), 1)

    def pick_rows(xs, part, first):
        span = 4 * SPOTS

        @pl.loop(0, Z)
        def _(q):
            at = pl.ds(pl.multiple_of(q * LIVE, LIVE), LIVE)
            spots = spot[at, :]
            tiles = []
            for t in range(span // 128):
                ends = []
                for s in (2 * t, 2 * t + 1):
                    ends.append((4 * part + s // 3) * X * SPOTS + (s % 3) * 64)
                there = jnp.where(lane < 64, lane + ends[0], lane - 64 + ends[1]) + xs * SPOTS
                tiles.append(one_hot(spots == there))
            got = dot(jnp.concatenate(tiles, axis=1), b_all[xs, part * span : (part + 1) * span, :])
            if first:
                picked[at, :] = got
            else:
                picked[at, :] += got

    ring(6)
    pick_rows(x, 0, True)
    pick_rows(x, 1, False)
    audio_relay()
    pick_rows(xmod(x - 1), 0, False)
    pick_rows(xmod(x - 1), 1, False)
    pick_rows(xmod(x + 1), 0, False)
    pick_rows(xmod(x + 1), 1, False)

    for t in range(3):
        for j in range(2):
            if (t + 1, j) not in up_items:
                arrived(a_rows(zmod(z - t - 1), j), "up", t, j)
            if (t + 1, j) not in down_items:
                arrived(a_rows(zmod(z + t + 1), j), "down", t, j)
    arrived(a_rows(zmod(z + 4), 0), "up", 3, 0)
    arrived(a_rows(zmod(z + 4), 1), "down", 3, 1)

    @pl.loop(0, Z)
    def _(zs):
        for j in range(2):
            a_t[:, pl.ds(pl.multiple_of(zs * LIVE + j * 128, 128), 128)] = a_all[
                zs, j * 128 : (j + 1) * 128, :
            ].T

    for k in range(Z):
        arrived(b_rows(xmod(x + 2), zmod(z - k)), "fr" if k < 4 else "fl", k)
    pick_rows(xmod(x + 2), 0, False)
    pick_rows(xmod(x + 2), 1, False)

    aud_part[...] = jnp.zeros_like(aud_part)
    sums = []
    for w in range(2):
        arrived(aud_recv.at[0, w], "aud3", w)
        arrived(aud_recv.at[1, 1 - w], "aud2", 1 - w)
        sums.append(audio_rows(x, w) + aud_recv[0, w].astype(f32) + aud_recv[1, 1 - w].astype(f32))
    audio[0 : 2 * EROWS, :] = jnp.concatenate(sums, axis=1)
    for zl in range(2):
        for d in range(Y * C):
            at = zl * EROWS + d * AROWS
            aud_part[zl, d, 0:AROWS, :] = audio[at : at + AROWS, :]

    picked_b[...] = picked[...].astype(bf16)
    other = 1 - core

    for zl in range(2):
        for m in range(2):
            at = pl.ds(zl * ZROWS + m * (ZROWS // 2), ZROWS // 2)
            merger[at, :] = dot(a_t[at, :], picked_b[...])

        def merger_rows(d):
            return merger[pl.ds(pl.multiple_of(zl * ZROWS + d * ROWS, 16), ROWS), :]

        for yt in range(Y):
            core_send[zl, yt, 0:ROWS, :] = merger_rows(2 * yt + other)
            core_send[zl, yt, ROWS:, :] = aud_part[zl, 2 * yt + other]
        send(core_send.at[zl], core_recv.at[zl], ("core", zl), {"core": other})
        for yt in range(Y):
            own[zl, yt, 0:ROWS, :] = merger_rows(2 * yt + core)
            own[zl, yt, ROWS:, :] = aud_part[zl, 2 * yt + core]

    y_sides = ((1, {"y": ymod(y + 1)}), (-1, {"y": ymod(y + Y - 1)}))

    def y_part(zl, yt, w):
        cols = slice(w * HALF, (w + 1) * HALF)
        return own[zl, yt, :, cols] + core_recv[zl, yt, :, cols]

    for zl in range(2):
        arrived(core_recv.at[zl], "core", zl)
        for w, (step, side) in enumerate(y_sides):
            y_send[zl, 0, w] = y_part(zl, ymod(y + 2), w).astype(bf16)
            send(y_send.at[zl, 0, w], y_relay.at[zl, w], ("y1", zl, w), side)
        for w, (step, side) in enumerate(y_sides):
            y_send[zl, 1, w] = y_part(zl, ymod(y + Y + step), 1 - w).astype(bf16)
            send(y_send.at[zl, 1, w], y_recv.at[zl, 1, w], ("y2", zl, w), side)
    for zl in range(2):
        for w, (step, side) in enumerate(y_sides):
            arrived(y_relay.at[zl, w], "y1", zl, w)
            y_send[zl, 2, w] = (y_part(zl, ymod(y + Y + step), w) + y_relay[zl, w].astype(f32)).astype(bf16)
            send(y_send.at[zl, 2, w], y_recv.at[zl, 0, w], ("y3", zl, w), side)

    fin = [(sem("fin", k), sem("fin", k + 2)) for k in (0, 1)]
    fin_out = [(sem("fout", k), sem("fout", k + 2)) for k in (0, 1)]
    assert fin[1][0] - fin[0][0] == 2

    def last(zl):
        device = {"z": x + X * zl, "x": home_x}
        return [
            pltpu.make_async_remote_copy(
                src_ref=src.at[zl], dst_ref=dst.at[half], send_sem=ssem.at[fin_out[zl][i]],
                recv_sem=rsem.at[fin[0][i] + 2 * half], device_id=device, device_id_type=MESH,
            )
            for i, (src, dst) in enumerate(((fin_send, fin_recv), (fina_send, fina_recv)))
        ]

    for zl in range(2):
        sums = []
        for w in range(2):
            arrived(y_recv.at[zl, 0, w], "y3", zl, w)
            arrived(y_recv.at[zl, 1, 1 - w], "y2", zl, 1 - w)
            sums.append(y_part(zl, y, w) + y_recv[zl, 0, w].astype(f32) + y_recv[zl, 1, 1 - w].astype(f32))
        total = jnp.concatenate(sums, axis=1)
        fin_send[zl] = total[0:ROWS].astype(bf16)
        fina_send[zl] = total[ROWS : ROWS + KEEP]
        elsewhere = jnp.logical_or(x + X * zl != z, home_x != x)

        @pl.when(elsewhere)
        def _():
            for c in last(zl):
                c.start()

        @pl.when(jnp.logical_not(elsewhere))
        def _():
            fin_recv[half] = fin_send[zl]
            fina_recv[half] = fina_send[zl]

    for h in range(2):
        @pl.when(jnp.logical_or(2 * x + h != z, lax.rem(z, X) != x))
        def _():
            for i, buffer in enumerate((fin_recv, fina_recv)):
                pltpu.make_async_remote_copy(
                    src_ref=buffer.at[h], dst_ref=buffer.at[h], send_sem=ssem.at[fin_out[0][i]],
                    recv_sem=rsem.at[fin[h][i]], device_id={"core": other}, device_id_type=MESH,
                ).wait_recv()

    out_m[:, 0:WIDE] = fin_recv[0].astype(f32)
    out_m[:, WIDE:] = fin_recv[1].astype(f32)[:, 2 * WIDE - BLOCK :]
    out_a[:, 0:WIDE] = fina_recv[0, 0:AROWS, :]
    out_a[:, WIDE:] = fina_recv[1, 0:AROWS, 2 * WIDE - BLOCK :]

    for c in sent:
        c.wait_send()
    for zl in range(2):

        @pl.when(jnp.logical_or(x + X * zl != z, home_x != x))
        def _():
            for c in last(zl):
                c.wait_send()

    assert len(names) <= 192


def local(mel, conv_weight, conv_bias, video_hidden, video_count, video_places, audio_places, cotangent):
    vmem = pl.BlockSpec(memory_space=pltpu.VMEM)
    hbm = pl.BlockSpec(memory_space=pl.ANY)
    part = (PART, WIDE)
    merger, audio = pl.pallas_call(
        kernel,
        out_shape=(
            jax.ShapeDtypeStruct((ROWS, BLOCK), f32),
            jax.ShapeDtypeStruct((AROWS, BLOCK), f32),
        ),
        in_specs=[vmem, vmem, vmem, hbm, vmem, vmem, vmem, hbm],
        out_specs=(vmem, vmem),
        scratch_shapes=[
            pltpu.VMEM((8, 128), i32),
            pltpu.VMEM((X, 8, 128), i32),
            pltpu.VMEM((X, Z, 8, 128), i32),
            pltpu.VMEM((X, Z, FRAMES, MELS), bf16),
            pltpu.VMEM((X, Z * SPOTS, WIDE), bf16),
            pltpu.VMEM((X, SLOTS, RROWS), bf16),
            pltpu.VMEM((Z, LIVE, RROWS), bf16),
            pltpu.VMEM((RROWS, Z * LIVE), bf16),
            pltpu.VMEM((X * Z * FRAMES, 4 * MELS), bf16),
            pltpu.VMEM((ENC, 4 * MELS), bf16),
            pltpu.VMEM((128, ENC), bf16),
            pltpu.VMEM((Z * LIVE, 128), i32),
            pltpu.VMEM((Z * LIVE, WIDE), f32),
            pltpu.VMEM((Z * LIVE, WIDE), bf16),
            pltpu.VMEM((RROWS, WIDE), f32),
            pltpu.VMEM((ENC, Z * SPOTS), bf16),
            pltpu.VMEM((ENC, WIDE), f32),
            pltpu.VMEM((3, 2, 2 * EROWS, HALF), bf16),
            pltpu.VMEM((2, 2 * EROWS, HALF), bf16),
            pltpu.VMEM((2, 2, 2 * EROWS, HALF), bf16),
            pltpu.VMEM((2, Y * C, APAD, WIDE), f32),
            pltpu.VMEM((2, Y, *part), f32),
            pltpu.VMEM((2, Y, *part), f32),
            pltpu.VMEM((2, Y, *part), f32),
            pltpu.VMEM((2, 3, 2, PART, HALF), bf16),
            pltpu.VMEM((2, 2, PART, HALF), bf16),
            pltpu.VMEM((2, 2, 2, PART, HALF), bf16),
            pltpu.VMEM((2, ROWS, WIDE), bf16),
            pltpu.VMEM((2, ROWS, WIDE), bf16),
            pltpu.VMEM((2, KEEP, WIDE), f32),
            pltpu.VMEM((2, KEEP, WIDE), f32),
            pltpu.VMEM((2, SLOTS, ZROWS), bf16),
            pltpu.VMEM((SPOTS // 2, WIDE), bf16),
            pltpu.SemaphoreType.DMA((192,)),
            pltpu.SemaphoreType.DMA((192,)),
        ],
        compiler_params=pltpu.CompilerParams(
            collective_id=0, has_side_effects=True, vmem_limit_bytes=60 * 2**20
        ),
    )(
        mel[0], conv_weight, conv_bias[None], video_hidden[0],
        video_count, video_places, audio_places, cotangent[0],
    )
    return merger[None], audio[None]


def solution(mesh):
    whole = Mesh(mesh.devices.reshape(Z, X, Y, C), ("z", "x", "y", "core"))
    dp, ctx = ("y", "core"), ("z", "x")
    return jax.shard_map(
        local,
        mesh=whole,
        in_specs=(
            P(dp, ctx, None),
            P(),
            P(),
            P(dp, ctx, None),
            P(dp, ctx),
            P(dp, ctx),
            P(dp, ctx),
            P(dp, ctx, None),
        ),
        out_specs=(P(ctx, dp, None), P(ctx, dp, None)),
        check_vma=False,
    )
```

```python
import jax
import jax.numpy as jnp
from jax import lax
from jax.experimental import pallas as pl
from jax.experimental.pallas import tpu as pltpu
from jax.sharding import Mesh, PartitionSpec as P

Z, X, Y, C = 8, 4, 4, 2
MELS, ENC, HID, OUT = 128, 1280, 5120, 3584
FRAMES, SLOTS, SPOTS = 128, 128, 192
BLOCK = OUT // X
WIDE = 512
RROWS = HID // X
ROWS = HID // Z // (Y * C)
AROWS = ENC // Z // (Y * C)
APAD = 32
PART = ROWS + APAD
KEEP = 24
HALF = 256
EROWS = ENC // Z
ZROWS = HID // Z
LIVE = 256

bf16, f32, i32 = jnp.bfloat16, jnp.float32, jnp.int32
MESH = pl.DeviceIdType.MESH


def dot(a, b, dims=((1,), (0,))):
    return lax.dot_general(a, b, (dims, ((), ())), preferred_element_type=f32)


def iota(shape, dim):
    return lax.broadcasted_iota(i32, shape, dim)


def one_hot(mask):
    return jnp.where(mask, 1.0, 0.0).astype(bf16)


def kernel(
    mel, convw, bias, hidden, count, vplaces, aplaces, cot,
    out_m, out_a,
    ints, ints_x, ints_all, mel_all, b_all, a_raw, a_all, a_t, windows, conv_t, w_ext,
    spot, picked, picked_b, merger, acts, audio, aud_send, aud_relay, aud_recv, aud_part, own, core_send, core_recv,
    y_send, y_relay, y_recv, fin_send, fin_recv, fina_send, fina_recv, a_relay, b_relay, ssem, rsem,
):
    z, x = lax.axis_index("z"), lax.axis_index("x")
    y, core = lax.axis_index("y"), lax.axis_index("core")

    def zmod(v):
        return lax.rem(v + 2 * Z, Z)

    def xmod(v):
        return lax.rem(v + 2 * X, X)

    def ymod(v):
        return lax.rem(v + Y, Y)

    home_x = lax.div(z, 2)
    half = lax.rem(z, 2)

    barrier = pltpu.get_barrier_semaphore()
    peers = [{"z": zmod(z + k)} for k in range(1, Z)]
    peers += [{"x": xmod(x + k)} for k in range(1, X)]
    peers += [{"y": ymod(y + k)} for k in range(1, Y)]
    peers += [{"core": 1 - core}]
    for peer in peers:
        pl.semaphore_signal(barrier, inc=1, device_id=peer, device_id_type=MESH)
    for h in range(2):

        @pl.when(jnp.logical_or(2 * x + h != z, lax.rem(z, X) != x))
        def _():
            pl.semaphore_signal(
                barrier, inc=1, device_id={"z": 2 * x + h, "x": lax.rem(z, X)}, device_id_type=MESH
            )

    here = jnp.logical_and(home_x == x, lax.rem(z, X) == x)
    pl.semaphore_wait(barrier, len(peers) + 2 - jnp.where(here, 1, 0))

    sent = []
    names = {}

    def sem(*key):
        return names.setdefault(key, len(names))

    def copy(src, dst, key, device):
        i = sem(*key)
        return pltpu.make_async_remote_copy(
            src_ref=src, dst_ref=dst, send_sem=ssem.at[i], recv_sem=rsem.at[i],
            device_id=device, device_id_type=MESH,
        )

    def send(src, dst, key, device):
        c = copy(src, dst, key, device)
        c.start()
        sent.append(c)

    def arrived(dst, *key):
        copy(dst, dst, key, {"core": 1 - core}).wait_recv()

    def window(zt):
        return pl.ds(pl.multiple_of(lax.div(zt, 2) * BLOCK + lax.rem(zt, 2) * (BLOCK - WIDE), 128), WIDE)

    def b_rows(xs, zs):
        return b_all.at[xs, pl.ds(pl.multiple_of(zs * SPOTS, 64), SPOTS)]

    def b_half(zs, h):
        return b_all.at[x, pl.ds(pl.multiple_of(zs * SPOTS + h * 96, 32), 96)]

    def a_cols(xt, w):
        return hidden.at[:, pl.ds(pl.multiple_of((xt + X * w) * ZROWS, 128), ZROWS)]

    def a_slot(xs, w):
        return a_raw.at[xs, :, pl.ds(w * ZROWS, ZROWS)]

    right, left = {"x": xmod(x + 1)}, {"x": xmod(x - 1)}
    sides = ((1, right), (-1, left))

    ints[0:1, :] = aplaces[...]
    ints[1:2, :] = vplaces[...]
    ints[2:3, :] = jnp.broadcast_to(count[...], (1, 128))
    ints[3:8, :] = jnp.zeros((5, 128), i32)
    ints_x[x] = ints[...]
    ints_all[x, z] = ints[...]
    mel_all[x, z] = mel[...]

    for k in range(1, Z):
        zt = zmod(z + k)
        send(ints, ints_all.at[x, z], ("iz", k), {"z": zt})
        send(mel, mel_all.at[x, z], ("mz", k), {"z": zt})
    for k in range(1, X):
        send(ints, ints_x.at[x], ("ix", k), {"x": xmod(x + k)})
    for w, (step, side) in enumerate(sides):
        send(a_cols(xmod(x + 2), w), a_relay.at[w], ("a2", w), side)
    for step, side in sides:
        for w in range(2):
            send(a_cols(xmod(x + step), w), a_slot(x, w), ("a", step, w), side)
    own_a = []
    for w in range(2):
        c = pltpu.make_async_copy(a_cols(x, w), a_slot(x, w), ssem.at[sem("own_a", w)])
        c.start()
        own_a.append(c)
    own_b = pltpu.make_async_copy(cot.at[:, window(z)], b_rows(x, z), ssem.at[sem("own_b")])
    own_b.start()
    zt = zmod(z + 4)
    send(cot.at[pl.ds(96, 96), window(zt)], b_relay, ("b4",), {"z": zmod(z - 1)})
    for k in (1, 7, 2, 6, 3, 5):
        zt = zmod(z + k)
        send(cot.at[:, window(zt)], b_rows(x, z), ("b", k), {"z": zt})
    zt = zmod(z + 4)
    send(cot.at[pl.ds(0, 96), window(zt)], b_half(z, 0), ("b", 4), {"z": zt})

    def b_out(k):
        block = b_rows(x, zmod(z - k))
        send(block, block, ("br", k), right)
        send(block, block, ("bl", k), left)


    def selection(held):
        row, col = iota((128, 256), 0), iota((128, 256), 1)
        return one_hot(jnp.where(row < held, row, row - held + 128) == col)

    up, down = {"z": zmod(z + 1)}, {"z": zmod(z - 1)}
    up_items = [(0, 0), (0, 1), (1, 0), (1, 1), (2, 0), (2, 1), (3, 0)]
    down_items = [(0, 0), (0, 1), (1, 0), (1, 1), (2, 0), (2, 1), (3, 1)]

    def pair(j):
        return lax.rem(lax.div(x, 2) + j, 2)

    def a_rows(zs, j):
        return a_all.at[zs, pl.ds(pl.multiple_of(pair(j) * 128, 128), 128)]

    def pack(j):
        p = pair(j)
        held = jnp.broadcast_to(ints_x[2 * p, 2:3, :][:, 0:1], (128, 256))
        both = jnp.concatenate([a_raw[2 * p], a_raw[2 * p + 1]], axis=0)
        a_all[z, pl.ds(pl.multiple_of(p * 128, 128), 128), :] = dot(selection(held), both).astype(bf16)

    def ring(n):
        for items, name, step, device in ((up_items, "up", -1, up), (down_items, "down", 1, down)):
            t, j = items[n]
            rows = a_rows(zmod(z + step * t), j)
            if t:
                arrived(rows, name, t - 1, j)
            send(rows, rows, (name, t, j), device)

    for w, (step, side) in enumerate(sides):
        arrived(a_relay.at[w], "a2", w)
        send(a_relay.at[w], a_slot(xmod(x - step), w), ("a3", w), side)
    own_b.wait()
    b_out(0)

    b0 = bias[...]
    hi = b0.astype(bf16).astype(f32)
    mid = (b0 - hi).astype(bf16).astype(f32)
    low = b0 - hi - mid
    row = iota((128, ENC), 0)
    w_ext[...] = jnp.where(row == 0, hi, jnp.where(row == 1, mid, jnp.where(row == 2, low, 0.0))).astype(bf16)
    conv_t[:, 0 : 3 * MELS] = convw[...].T
    conv_t[:, 3 * MELS :] = w_ext[...].T

    for k in range(1, Z):
        arrived(ints_all.at[x, zmod(z - k)], "iz", k)
        arrived(mel_all.at[x, zmod(z - k)], "mz", k)
    def mel_half(xs, w):
        return mel_all.at[xs, pl.ds(w * (Z // 2), Z // 2)]

    for k in range(1, X):
        send(ints_all.at[x], ints_all.at[x], ("ixa", k), {"x": xmod(x + k)})
    for w in range(2):
        for step, side in sides:
            send(mel_half(x, w), mel_half(x, w), ("mxa", step, w), side)

    for c in own_a:
        c.wait()
    for k in range(1, X):
        arrived(ints_x.at[xmod(x - k)], "ix", k)
    for w, (step, side) in enumerate(sides):
        for v in range(2):
            arrived(a_slot(xmod(x - step), v), "a", step, v)
    pack(0)
    ring(0)
    for w in range(2):
        arrived(a_slot(xmod(x + 2), w), "a3", w)
    pack(1)
    ring(1)

    def forward(ks):
        for k in ks:
            zs = zmod(z - k)
            block = b_rows(xmod(x - 1), zs)
            arrived(block, "br", k)
            if k < 4:
                send(block, block, ("fr", k), right)
            block = b_rows(xmod(x + 1), zs)
            arrived(block, "bl", k)
            if k >= 4:
                send(block, block, ("fl", k), left)

    def audio_piece(h):
        wpos = []
        for zs in (2 * h, 2 * h + 1):
            base = (zs * X + x) * SPOTS
            here = iota((SPOTS, 128), 0) + base
            total = jnp.zeros((SPOTS, 4 * MELS), f32)

            def shard(xs, total):
                hot = jnp.concatenate(
                    [
                        one_hot(jnp.broadcast_to(ints_all[xs, zt, 0:1, :], (SPOTS, 128)) == here)
                        for zt in range(Z)
                    ],
                    axis=1,
                )
                at = pl.ds(pl.multiple_of(xs * (Z * FRAMES), FRAMES), Z * FRAMES)
                return total + dot(hot, windows[at, :])

            wpos.append(lax.fori_loop(0, X, shard, total).astype(bf16))
        wpos = jnp.concatenate(wpos, axis=0)

        @pl.loop(0, ENC // 256)
        def _(m):
            at = pl.ds(pl.multiple_of(m * 256, 256), 256)
            conv = dot(conv_t[at, :], wpos, ((1,), (1,)))
            act = (0.5 * conv * (1.0 + lax.erf(conv * 0.7071067811865476))).astype(bf16)
            acts[at, h * 2 * SPOTS : (h + 1) * 2 * SPOTS] = act

    def b_in(ks):
        for k in ks:
            arrived(b_rows(x, zmod(z - k)), "b", k)
            b_out(k)

    for w, (step, side) in enumerate(sides):
        rows = mel_half(xmod(x - step), w)
        arrived(rows, "mxa", step, w)
        send(rows, rows, ("mxb", w), side)
    arrived(b_relay, "b4")
    send(b_relay, b_half(zmod(z + 1), 1), ("b5",), {"z": zmod(z - 3)})
    for k in (1, 7):
        arrived(b_rows(x, zmod(z - k)), "b", k)
        b_out(k)

    forward((0,))
    for k in range(1, X):
        arrived(ints_all.at[xmod(x - k)], "ixa", k)
    for w, (step, side) in enumerate(sides):
        arrived(mel_half(xmod(x - step), 1 - w), "mxa", step, 1 - w)
        arrived(mel_half(xmod(x + 2), w), "mxb", w)

    windows[:, 3 * MELS :] = jnp.ones((X * Z * FRAMES, 128), bf16)
    edge = iota((FRAMES, MELS), 0)

    @pl.loop(0, Z)
    def _(zs):
        for xs in range(X):
            own_frames = mel_all[xs, zs].astype(f32)
            zp = zs if xs else jnp.maximum(zs - 1, 0)
            zn = zs if xs < X - 1 else jnp.minimum(zs + 1, Z - 1)
            before = mel_all[(xs - 1) % X, zp].astype(f32)
            after = mel_all[(xs + 1) % X, zn].astype(f32)
            if xs == 0:
                before = jnp.where(jnp.broadcast_to(zs, before.shape) == 0, 0.0, before)
            if xs == X - 1:
                after = jnp.where(jnp.broadcast_to(zs, after.shape) == Z - 1, 0.0, after)
            before = jnp.where(edge == 0, pltpu.roll(before, 1, 0), pltpu.roll(own_frames, 1, 0))
            after = jnp.where(
                edge == FRAMES - 1, pltpu.roll(after, FRAMES - 1, 0), pltpu.roll(own_frames, FRAMES - 1, 0)
            )
            at = pl.ds(pl.multiple_of((xs * Z + zs) * FRAMES, FRAMES), FRAMES)
            windows[at, 0:MELS] = before.astype(bf16)
            windows[at, MELS : 2 * MELS] = own_frames.astype(bf16)
            windows[at, 2 * MELS : 3 * MELS] = after.astype(bf16)

    b_in((2, 6))

    @pl.loop(0, Z)
    def _(zs):
        for j in range(2):
            held = jnp.broadcast_to(ints_all[2 * j, zs, 2:3, :][:, 0:1], (128, 256))
            pick = selection(held)
            places = jnp.concatenate([ints_all[2 * j, zs, 1:2, :], ints_all[2 * j + 1, zs, 1:2, :]], axis=1)
            high = lax.shift_right_logical(places, 7)
            rest = jnp.bitwise_and(places, 127)
            high = jnp.broadcast_to(high.astype(f32), (128, 256)).astype(bf16)
            rest = jnp.broadcast_to(rest.astype(f32), (128, 256)).astype(bf16)
            value = 128.0 * dot(pick, high, ((1,), (1,))) + dot(pick, rest, ((1,), (1,)))
            spot[pl.ds(pl.multiple_of(zs * LIVE + j * 128, 128), 128), :] = value.astype(i32)

    lane = iota((256, 128), 1)

    def pick_rows(xs, part, first):
        span = 4 * SPOTS

        @pl.loop(0, Z)
        def _(q):
            at = pl.ds(pl.multiple_of(q * LIVE, LIVE), LIVE)
            spots = spot[at, :]
            tiles = []
            for t in range(span // 128):
                ends = []
                for s in (2 * t, 2 * t + 1):
                    ends.append((4 * part + s // 3) * X * SPOTS + (s % 3) * 64)
                there = jnp.where(lane < 64, lane + ends[0], lane - 64 + ends[1]) + xs * SPOTS
                tiles.append(one_hot(spots == there))
            got = dot(jnp.concatenate(tiles, axis=1), b_all[xs, part * span : (part + 1) * span, :])
            if first:
                picked[at, :] = got
            else:
                picked[at, :] += got

    ring(2)
    b_in((3, 5))
    forward((1, 7))
    audio_piece(0)
    arrived(b_half(zmod(z - 4), 0), "b", 4)
    arrived(b_half(zmod(z + 4), 1), "b5")
    b_out(4)
    forward((2, 6))
    audio_piece(1)
    ring(3)
    forward((3,))
    pick_rows(x, 0, True)
    audio_piece(2)
    ring(4)
    forward((5, 4))
    audio_piece(3)

    @pl.loop(0, ENC // 256)
    def _(m):
        at = pl.ds(pl.multiple_of(m * 256, 256), 256)
        audio[at, :] = dot(acts[at, :], b_all[x])

    def audio_rows(xt, w):
        rows = [
            audio[pl.ds(pl.multiple_of((xt + X * zl) * EROWS, 32), EROWS), w * HALF : (w + 1) * HALF]
            for zl in range(2)
        ]
        return jnp.concatenate(rows, axis=0)

    for w, (step, side) in enumerate(sides):
        aud_send[0, w] = audio_rows(xmod(x + 2), w).astype(bf16)
        send(aud_send.at[0, w], aud_relay.at[w], ("aud1", w), side)
        aud_send[1, w] = audio_rows(xmod(x + step), 1 - w).astype(bf16)
        send(aud_send.at[1, w], aud_recv.at[1, w], ("aud2", w), side)

    def audio_relay():
        for w, (step, side) in enumerate(sides):
            arrived(aud_relay.at[w], "aud1", w)
            aud_send[2, w] = (audio_rows(xmod(x + step), w) + aud_relay[w].astype(f32)).astype(bf16)
            send(aud_send.at[2, w], aud_recv.at[0, w], ("aud3", w), side)

    def turn(first, last):
        @pl.loop(first, last)
        def _(i):
            zs = zmod(z + i)
            for j in range(2):
                a_t[:, pl.ds(pl.multiple_of(zs * LIVE + j * 128, 128), 128)] = a_all[
                    zs, j * 128 : (j + 1) * 128, :
                ].T

    pick_rows(x, 1, False)
    ring(5)
    pick_rows(xmod(x - 1), 0, False)
    pick_rows(xmod(x - 1), 1, False)
    ring(6)
    audio_relay()
    pick_rows(xmod(x + 1), 0, False)
    pick_rows(xmod(x + 1), 1, False)
    turn(-2, 3)
    for k in range(Z):
        arrived(b_rows(xmod(x + 2), zmod(z - k)), "fr" if k < 4 else "fl", k)
    pick_rows(xmod(x + 2), 0, False)
    pick_rows(xmod(x + 2), 1, False)

    for t in range(3):
        for j in range(2):
            if (t + 1, j) not in up_items:
                arrived(a_rows(zmod(z - t - 1), j), "up", t, j)
            if (t + 1, j) not in down_items:
                arrived(a_rows(zmod(z + t + 1), j), "down", t, j)
    arrived(a_rows(zmod(z + 4), 0), "up", 3, 0)
    arrived(a_rows(zmod(z + 4), 1), "down", 3, 1)
    turn(3, 6)

    aud_part[...] = jnp.zeros_like(aud_part)
    sums = []
    for w in range(2):
        arrived(aud_recv.at[0, w], "aud3", w)
        arrived(aud_recv.at[1, 1 - w], "aud2", 1 - w)
        sums.append(audio_rows(x, w) + aud_recv[0, w].astype(f32) + aud_recv[1, 1 - w].astype(f32))
    audio[0 : 2 * EROWS, :] = jnp.concatenate(sums, axis=1)
    for zl in range(2):
        for d in range(Y * C):
            at = zl * EROWS + d * AROWS
            aud_part[zl, d, 0:AROWS, :] = audio[at : at + AROWS, :]

    picked_b[...] = picked[...].astype(bf16)
    other = 1 - core

    for zl in range(2):
        for m in range(2):
            at = pl.ds(zl * ZROWS + m * (ZROWS // 2), ZROWS // 2)
            merger[at, :] = dot(a_t[at, :], picked_b[...])

        def merger_rows(d):
            return merger[pl.ds(pl.multiple_of(zl * ZROWS + d * ROWS, 16), ROWS), :]

        for yt in range(Y):
            core_send[zl, yt, 0:ROWS, :] = merger_rows(2 * yt + other)
            core_send[zl, yt, ROWS:, :] = aud_part[zl, 2 * yt + other]
        send(core_send.at[zl], core_recv.at[zl], ("core", zl), {"core": other})
        for yt in range(Y):
            own[zl, yt, 0:ROWS, :] = merger_rows(2 * yt + core)
            own[zl, yt, ROWS:, :] = aud_part[zl, 2 * yt + core]

    y_sides = ((1, {"y": ymod(y + 1)}), (-1, {"y": ymod(y + Y - 1)}))

    def y_part(zl, yt, w):
        cols = slice(w * HALF, (w + 1) * HALF)
        return own[zl, yt, :, cols] + core_recv[zl, yt, :, cols]

    for zl in range(2):
        arrived(core_recv.at[zl], "core", zl)
        for w, (step, side) in enumerate(y_sides):
            y_send[zl, 0, w] = y_part(zl, ymod(y + 2), w).astype(bf16)
            send(y_send.at[zl, 0, w], y_relay.at[zl, w], ("y1", zl, w), side)
        for w, (step, side) in enumerate(y_sides):
            y_send[zl, 1, w] = y_part(zl, ymod(y + Y + step), 1 - w).astype(bf16)
            send(y_send.at[zl, 1, w], y_recv.at[zl, 1, w], ("y2", zl, w), side)
    for zl in range(2):
        for w, (step, side) in enumerate(y_sides):
            arrived(y_relay.at[zl, w], "y1", zl, w)
            y_send[zl, 2, w] = (y_part(zl, ymod(y + Y + step), w) + y_relay[zl, w].astype(f32)).astype(bf16)
            send(y_send.at[zl, 2, w], y_recv.at[zl, 0, w], ("y3", zl, w), side)

    fin = [(sem("fin", k), sem("fin", k + 2)) for k in (0, 1)]
    fin_out = [(sem("fout", k), sem("fout", k + 2)) for k in (0, 1)]
    assert fin[1][0] - fin[0][0] == 2

    def last(zl):
        device = {"z": x + X * zl, "x": home_x}
        return [
            pltpu.make_async_remote_copy(
                src_ref=src.at[zl], dst_ref=dst.at[half], send_sem=ssem.at[fin_out[zl][i]],
                recv_sem=rsem.at[fin[0][i] + 2 * half], device_id=device, device_id_type=MESH,
            )
            for i, (src, dst) in enumerate(((fin_send, fin_recv), (fina_send, fina_recv)))
        ]

    for zl in range(2):
        sums = []
        for w in range(2):
            arrived(y_recv.at[zl, 0, w], "y3", zl, w)
            arrived(y_recv.at[zl, 1, 1 - w], "y2", zl, 1 - w)
            sums.append(y_part(zl, y, w) + y_recv[zl, 0, w].astype(f32) + y_recv[zl, 1, 1 - w].astype(f32))
        total = jnp.concatenate(sums, axis=1)
        fin_send[zl] = total[0:ROWS].astype(bf16)
        fina_send[zl] = total[ROWS : ROWS + KEEP]
        elsewhere = jnp.logical_or(x + X * zl != z, home_x != x)

        @pl.when(elsewhere)
        def _():
            for c in last(zl):
                c.start()

        @pl.when(jnp.logical_not(elsewhere))
        def _():
            fin_recv[half] = fin_send[zl]
            fina_recv[half] = fina_send[zl]

    for h in range(2):
        @pl.when(jnp.logical_or(2 * x + h != z, lax.rem(z, X) != x))
        def _():
            for i, buffer in enumerate((fin_recv, fina_recv)):
                pltpu.make_async_remote_copy(
                    src_ref=buffer.at[h], dst_ref=buffer.at[h], send_sem=ssem.at[fin_out[0][i]],
                    recv_sem=rsem.at[fin[h][i]], device_id={"core": other}, device_id_type=MESH,
                ).wait_recv()

    out_m[:, 0:WIDE] = fin_recv[0].astype(f32)
    out_m[:, WIDE:] = fin_recv[1].astype(f32)[:, 2 * WIDE - BLOCK :]
    out_a[:, 0:WIDE] = fina_recv[0, 0:AROWS, :]
    out_a[:, WIDE:] = fina_recv[1, 0:AROWS, 2 * WIDE - BLOCK :]

    for c in sent:
        c.wait_send()
    for zl in range(2):

        @pl.when(jnp.logical_or(x + X * zl != z, home_x != x))
        def _():
            for c in last(zl):
                c.wait_send()

    assert len(names) <= 192


def local(mel, conv_weight, conv_bias, video_hidden, video_count, video_places, audio_places, cotangent):
    vmem = pl.BlockSpec(memory_space=pltpu.VMEM)
    hbm = pl.BlockSpec(memory_space=pl.ANY)
    part = (PART, WIDE)
    merger, audio = pl.pallas_call(
        kernel,
        out_shape=(
            jax.ShapeDtypeStruct((ROWS, BLOCK), f32),
            jax.ShapeDtypeStruct((AROWS, BLOCK), f32),
        ),
        in_specs=[vmem, vmem, vmem, hbm, vmem, vmem, vmem, hbm],
        out_specs=(vmem, vmem),
        scratch_shapes=[
            pltpu.VMEM((8, 128), i32),
            pltpu.VMEM((X, 8, 128), i32),
            pltpu.VMEM((X, Z, 8, 128), i32),
            pltpu.VMEM((X, Z, FRAMES, MELS), bf16),
            pltpu.VMEM((X, Z * SPOTS, WIDE), bf16),
            pltpu.VMEM((X, SLOTS, RROWS), bf16),
            pltpu.VMEM((Z, LIVE, RROWS), bf16),
            pltpu.VMEM((RROWS, Z * LIVE), bf16),
            pltpu.VMEM((X * Z * FRAMES, 4 * MELS), bf16),
            pltpu.VMEM((ENC, 4 * MELS), bf16),
            pltpu.VMEM((128, ENC), bf16),
            pltpu.VMEM((Z * LIVE, 128), i32),
            pltpu.VMEM((Z * LIVE, WIDE), f32),
            pltpu.VMEM((Z * LIVE, WIDE), bf16),
            pltpu.VMEM((RROWS, WIDE), f32),
            pltpu.VMEM((ENC, Z * SPOTS), bf16),
            pltpu.VMEM((ENC, WIDE), f32),
            pltpu.VMEM((3, 2, 2 * EROWS, HALF), bf16),
            pltpu.VMEM((2, 2 * EROWS, HALF), bf16),
            pltpu.VMEM((2, 2, 2 * EROWS, HALF), bf16),
            pltpu.VMEM((2, Y * C, APAD, WIDE), f32),
            pltpu.VMEM((2, Y, *part), f32),
            pltpu.VMEM((2, Y, *part), f32),
            pltpu.VMEM((2, Y, *part), f32),
            pltpu.VMEM((2, 3, 2, PART, HALF), bf16),
            pltpu.VMEM((2, 2, PART, HALF), bf16),
            pltpu.VMEM((2, 2, 2, PART, HALF), bf16),
            pltpu.VMEM((2, ROWS, WIDE), bf16),
            pltpu.VMEM((2, ROWS, WIDE), bf16),
            pltpu.VMEM((2, KEEP, WIDE), f32),
            pltpu.VMEM((2, KEEP, WIDE), f32),
            pltpu.VMEM((2, SLOTS, ZROWS), bf16),
            pltpu.VMEM((SPOTS // 2, WIDE), bf16),
            pltpu.SemaphoreType.DMA((192,)),
            pltpu.SemaphoreType.DMA((192,)),
        ],
        compiler_params=pltpu.CompilerParams(
            collective_id=0, has_side_effects=True, vmem_limit_bytes=60 * 2**20
        ),
    )(
        mel[0], conv_weight, conv_bias[None], video_hidden[0],
        video_count, video_places, audio_places, cotangent[0],
    )
    return merger[None], audio[None]


def solution(mesh):
    whole = Mesh(mesh.devices.reshape(Z, X, Y, C), ("z", "x", "y", "core"))
    dp, ctx = ("y", "core"), ("z", "x")
    return jax.shard_map(
        local,
        mesh=whole,
        in_specs=(
            P(dp, ctx, None),
            P(),
            P(),
            P(dp, ctx, None),
            P(dp, ctx),
            P(dp, ctx),
            P(dp, ctx),
            P(dp, ctx, None),
        ),
        out_specs=(P(ctx, dp, None), P(ctx, dp, None)),
        check_vma=False,
    )
```

```python
import jax
import jax.numpy as jnp
from jax import lax
from jax.experimental import pallas as pl
from jax.experimental.pallas import tpu as pltpu
from jax.sharding import Mesh, PartitionSpec as P

Z, X, Y, C = 8, 4, 4, 2
MELS, ENC, HID, OUT = 128, 1280, 5120, 3584
FRAMES, SLOTS, SPOTS = 128, 128, 192
BLOCK = OUT // X
WIDE = 512
RROWS = HID // X
ROWS = HID // Z // (Y * C)
AROWS = ENC // Z // (Y * C)
APAD = 32
PART = ROWS + APAD
KEEP = 24
HALF = 256
EROWS = ENC // Z
ZROWS = HID // Z
LIVE = 256

bf16, f32, i32 = jnp.bfloat16, jnp.float32, jnp.int32
MESH = pl.DeviceIdType.MESH


def dot(a, b, dims=((1,), (0,))):
    return lax.dot_general(a, b, (dims, ((), ())), preferred_element_type=f32)


def iota(shape, dim):
    return lax.broadcasted_iota(i32, shape, dim)


def one_hot(mask):
    return jnp.where(mask, 1.0, 0.0).astype(bf16)


def kernel(
    mel, convw, bias, hidden, count, vplaces, aplaces, cot,
    out_m, out_a,
    ints, ints_x, ints_all, mel_all, b_all, a_raw, a_all, a_t, windows, conv_t, w_ext,
    spot, picked, picked_b, merger, acts, audio, aud_send, aud_relay, aud_recv, aud_part, own, core_send, core_recv,
    y_send, y_relay, y_recv, fin_send, fin_recv, fina_send, fina_recv, a_relay, b_relay, ssem, rsem,
):
    z, x = lax.axis_index("z"), lax.axis_index("x")
    y, core = lax.axis_index("y"), lax.axis_index("core")

    def zmod(v):
        return lax.rem(v + 2 * Z, Z)

    def xmod(v):
        return lax.rem(v + 2 * X, X)

    def ymod(v):
        return lax.rem(v + Y, Y)

    home_x = lax.div(z, 2)
    half = lax.rem(z, 2)

    barrier = pltpu.get_barrier_semaphore()
    peers = [{"z": zmod(z + k)} for k in range(1, Z)]
    peers += [{"x": xmod(x + k)} for k in range(1, X)]
    peers += [{"y": ymod(y + k)} for k in range(1, Y)]
    peers += [{"core": 1 - core}]
    for peer in peers:
        pl.semaphore_signal(barrier, inc=1, device_id=peer, device_id_type=MESH)
    for h in range(2):

        @pl.when(jnp.logical_or(2 * x + h != z, lax.rem(z, X) != x))
        def _():
            pl.semaphore_signal(
                barrier, inc=1, device_id={"z": 2 * x + h, "x": lax.rem(z, X)}, device_id_type=MESH
            )

    here = jnp.logical_and(home_x == x, lax.rem(z, X) == x)
    pl.semaphore_wait(barrier, len(peers) + 2 - jnp.where(here, 1, 0))

    sent = []
    names = {}

    def sem(*key):
        return names.setdefault(key, len(names))

    def copy(src, dst, key, device):
        i = sem(*key)
        return pltpu.make_async_remote_copy(
            src_ref=src, dst_ref=dst, send_sem=ssem.at[i], recv_sem=rsem.at[i],
            device_id=device, device_id_type=MESH,
        )

    def send(src, dst, key, device):
        c = copy(src, dst, key, device)
        c.start()
        sent.append(c)

    def arrived(dst, *key):
        copy(dst, dst, key, {"core": 1 - core}).wait_recv()

    def window(zt):
        return pl.ds(pl.multiple_of(lax.div(zt, 2) * BLOCK + lax.rem(zt, 2) * (BLOCK - WIDE), 128), WIDE)

    def b_rows(xs, zs):
        return b_all.at[xs, pl.ds(pl.multiple_of(zs * SPOTS, 64), SPOTS)]

    def b_half(zs, h):
        return b_all.at[x, pl.ds(pl.multiple_of(zs * SPOTS + h * 96, 32), 96)]

    def a_cols(xt, w):
        return hidden.at[:, pl.ds(pl.multiple_of((xt + X * w) * ZROWS, 128), ZROWS)]

    def a_slot(xs, w):
        return a_raw.at[xs, :, pl.ds(w * ZROWS, ZROWS)]

    right, left = {"x": xmod(x + 1)}, {"x": xmod(x - 1)}
    sides = ((1, right), (-1, left))

    ints[0:1, :] = aplaces[...]
    ints[1:2, :] = vplaces[...]
    ints[2:3, :] = jnp.broadcast_to(count[...], (1, 128))
    ints[3:8, :] = jnp.zeros((5, 128), i32)
    ints_x[x] = ints[...]
    ints_all[x, z] = ints[...]
    mel_all[x, z] = mel[...]

    for k in range(1, Z):
        zt = zmod(z + k)
        send(ints, ints_all.at[x, z], ("iz", k), {"z": zt})
        send(mel, mel_all.at[x, z], ("mz", k), {"z": zt})
    for k in range(1, X):
        send(ints, ints_x.at[x], ("ix", k), {"x": xmod(x + k)})
    for w, (step, side) in enumerate(sides):
        send(a_cols(xmod(x + 2), w), a_relay.at[w], ("a2", w), side)
    for step, side in sides:
        for w in range(2):
            send(a_cols(xmod(x + step), w), a_slot(x, w), ("a", step, w), side)
    own_a = []
    for w in range(2):
        c = pltpu.make_async_copy(a_cols(x, w), a_slot(x, w), ssem.at[sem("own_a", w)])
        c.start()
        own_a.append(c)
    own_b = pltpu.make_async_copy(cot.at[:, window(z)], b_rows(x, z), ssem.at[sem("own_b")])
    own_b.start()
    zt = zmod(z + 4)
    send(cot.at[pl.ds(96, 96), window(zt)], b_relay, ("b4",), {"z": zmod(z - 1)})
    for k in (1, 7, 2, 6, 3, 5):
        zt = zmod(z + k)
        send(cot.at[:, window(zt)], b_rows(x, z), ("b", k), {"z": zt})
    zt = zmod(z + 4)
    send(cot.at[pl.ds(0, 96), window(zt)], b_half(z, 0), ("b", 4), {"z": zt})

    def b_out(k):
        block = b_rows(x, zmod(z - k))
        send(block, block, ("br", k), right)
        send(block, block, ("bl", k), left)


    def selection(held):
        row, col = iota((128, 256), 0), iota((128, 256), 1)
        return one_hot(jnp.where(row < held, row, row - held + 128) == col)

    up, down = {"z": zmod(z + 1)}, {"z": zmod(z - 1)}
    up_items = [(0, 0), (0, 1), (1, 0), (1, 1), (2, 0), (2, 1), (3, 0)]
    down_items = [(0, 0), (0, 1), (1, 0), (1, 1), (2, 0), (2, 1), (3, 1)]

    def pair(j):
        return lax.rem(lax.div(x, 2) + j, 2)

    def a_rows(zs, j):
        return a_all.at[zs, pl.ds(pl.multiple_of(pair(j) * 128, 128), 128)]

    def pack(j):
        p = pair(j)
        held = jnp.broadcast_to(ints_x[2 * p, 2:3, :][:, 0:1], (128, 256))
        both = jnp.concatenate([a_raw[2 * p], a_raw[2 * p + 1]], axis=0)
        a_all[z, pl.ds(pl.multiple_of(p * 128, 128), 128), :] = dot(selection(held), both).astype(bf16)

    def ring(n):
        for items, name, step, device in ((up_items, "up", -1, up), (down_items, "down", 1, down)):
            t, j = items[n]
            rows = a_rows(zmod(z + step * t), j)
            if t:
                arrived(rows, name, t - 1, j)
            send(rows, rows, (name, t, j), device)

    for w, (step, side) in enumerate(sides):
        arrived(a_relay.at[w], "a2", w)
        send(a_relay.at[w], a_slot(xmod(x - step), w), ("a3", w), side)
    own_b.wait()
    b_out(0)

    b0 = bias[...]
    hi = b0.astype(bf16).astype(f32)
    mid = (b0 - hi).astype(bf16).astype(f32)
    low = b0 - hi - mid
    row = iota((128, ENC), 0)
    w_ext[...] = jnp.where(row == 0, hi, jnp.where(row == 1, mid, jnp.where(row == 2, low, 0.0))).astype(bf16)
    conv_t[:, 0 : 3 * MELS] = convw[...].T
    conv_t[:, 3 * MELS :] = w_ext[...].T

    for k in range(1, Z):
        arrived(ints_all.at[x, zmod(z - k)], "iz", k)
        arrived(mel_all.at[x, zmod(z - k)], "mz", k)
    def mel_half(xs, w):
        return mel_all.at[xs, pl.ds(w * (Z // 2), Z // 2)]

    for k in range(1, X):
        send(ints_all.at[x], ints_all.at[x], ("ixa", k), {"x": xmod(x + k)})
    for w in range(2):
        for step, side in sides:
            send(mel_half(x, w), mel_half(x, w), ("mxa", step, w), side)

    for c in own_a:
        c.wait()
    for k in range(1, X):
        arrived(ints_x.at[xmod(x - k)], "ix", k)
    for w, (step, side) in enumerate(sides):
        for v in range(2):
            arrived(a_slot(xmod(x - step), v), "a", step, v)
    pack(0)
    ring(0)
    for w in range(2):
        arrived(a_slot(xmod(x + 2), w), "a3", w)
    pack(1)
    ring(1)

    def forward(ks):
        for k in ks:
            zs = zmod(z - k)
            block = b_rows(xmod(x - 1), zs)
            arrived(block, "br", k)
            if k < 4:
                send(block, block, ("fr", k), right)
            block = b_rows(xmod(x + 1), zs)
            arrived(block, "bl", k)
            if k >= 4:
                send(block, block, ("fl", k), left)

    def audio_piece(h):
        wpos = []
        for zs in (2 * h, 2 * h + 1):
            base = (zs * X + x) * SPOTS
            here = iota((SPOTS, 128), 0) + base
            total = jnp.zeros((SPOTS, 4 * MELS), f32)

            def shard(xs, total):
                hot = jnp.concatenate(
                    [
                        one_hot(jnp.broadcast_to(ints_all[xs, zt, 0:1, :], (SPOTS, 128)) == here)
                        for zt in range(Z)
                    ],
                    axis=1,
                )
                at = pl.ds(pl.multiple_of(xs * (Z * FRAMES), FRAMES), Z * FRAMES)
                return total + dot(hot, windows[at, :])

            wpos.append(lax.fori_loop(0, X, shard, total).astype(bf16))
        wpos = jnp.concatenate(wpos, axis=0)

        @pl.loop(0, ENC // 256)
        def _(m):
            at = pl.ds(pl.multiple_of(m * 256, 256), 256)
            conv = dot(conv_t[at, :], wpos, ((1,), (1,)))
            act = (0.5 * conv * (1.0 + lax.erf(conv * 0.7071067811865476))).astype(bf16)
            acts[at, h * 2 * SPOTS : (h + 1) * 2 * SPOTS] = act

    def b_in(ks):
        for k in ks:
            arrived(b_rows(x, zmod(z - k)), "b", k)
            b_out(k)

    for w, (step, side) in enumerate(sides):
        rows = mel_half(xmod(x - step), w)
        arrived(rows, "mxa", step, w)
        send(rows, rows, ("mxb", w), side)
    arrived(b_relay, "b4")
    send(b_relay, b_half(zmod(z + 1), 1), ("b5",), {"z": zmod(z - 3)})
    for k in (1, 7):
        arrived(b_rows(x, zmod(z - k)), "b", k)
        b_out(k)

    forward((0,))
    for k in range(1, X):
        arrived(ints_all.at[xmod(x - k)], "ixa", k)
    for w, (step, side) in enumerate(sides):
        arrived(mel_half(xmod(x - step), 1 - w), "mxa", step, 1 - w)
        arrived(mel_half(xmod(x + 2), w), "mxb", w)

    windows[:, 3 * MELS :] = jnp.ones((X * Z * FRAMES, 128), bf16)
    edge = iota((FRAMES, MELS), 0)

    @pl.loop(0, Z)
    def _(zs):
        for xs in range(X):
            own_frames = mel_all[xs, zs].astype(f32)
            zp = zs if xs else jnp.maximum(zs - 1, 0)
            zn = zs if xs < X - 1 else jnp.minimum(zs + 1, Z - 1)
            before = mel_all[(xs - 1) % X, zp].astype(f32)
            after = mel_all[(xs + 1) % X, zn].astype(f32)
            if xs == 0:
                before = jnp.where(jnp.broadcast_to(zs, before.shape) == 0, 0.0, before)
            if xs == X - 1:
                after = jnp.where(jnp.broadcast_to(zs, after.shape) == Z - 1, 0.0, after)
            before = jnp.where(edge == 0, pltpu.roll(before, 1, 0), pltpu.roll(own_frames, 1, 0))
            after = jnp.where(
                edge == FRAMES - 1, pltpu.roll(after, FRAMES - 1, 0), pltpu.roll(own_frames, FRAMES - 1, 0)
            )
            at = pl.ds(pl.multiple_of((xs * Z + zs) * FRAMES, FRAMES), FRAMES)
            windows[at, 0:MELS] = before.astype(bf16)
            windows[at, MELS : 2 * MELS] = own_frames.astype(bf16)
            windows[at, 2 * MELS : 3 * MELS] = after.astype(bf16)

    b_in((2, 6))

    @pl.loop(0, Z)
    def _(zs):
        for j in range(2):
            held = jnp.broadcast_to(ints_all[2 * j, zs, 2:3, :][:, 0:1], (128, 256))
            pick = selection(held)
            places = jnp.concatenate([ints_all[2 * j, zs, 1:2, :], ints_all[2 * j + 1, zs, 1:2, :]], axis=1)
            high = lax.shift_right_logical(places, 7)
            rest = jnp.bitwise_and(places, 127)
            high = jnp.broadcast_to(high.astype(f32), (128, 256)).astype(bf16)
            rest = jnp.broadcast_to(rest.astype(f32), (128, 256)).astype(bf16)
            value = 128.0 * dot(pick, high, ((1,), (1,))) + dot(pick, rest, ((1,), (1,)))
            spot[pl.ds(pl.multiple_of(zs * LIVE + j * 128, 128), 128), :] = value.astype(i32)

    lane = iota((256, 128), 1)

    def pick_rows(xs, parts, first=False, last=False):
        span = 4 * SPOTS
        blocks = pl.ds(parts[0] * span, len(parts) * span)

        @pl.loop(0, Z)
        def _(q):
            at = pl.ds(pl.multiple_of(q * LIVE, LIVE), LIVE)
            spots = spot[at, :]
            tiles = []
            for part in parts:
                for t in range(span // 128):
                    ends = []
                    for s in (2 * t, 2 * t + 1):
                        ends.append((4 * part + s // 3) * X * SPOTS + (s % 3) * 64)
                    there = jnp.where(lane < 64, lane + ends[0], lane - 64 + ends[1]) + xs * SPOTS
                    tiles.append(one_hot(spots == there))
            got = dot(jnp.concatenate(tiles, axis=1), b_all[xs, blocks, :])
            if last:
                picked_b[at, :] = (picked[at, :] + got).astype(bf16)
            elif first:
                picked[at, :] = got
            else:
                picked[at, :] += got

    ring(2)
    b_in((3, 5))
    forward((1, 7))
    audio_piece(0)
    arrived(b_half(zmod(z - 4), 0), "b", 4)
    arrived(b_half(zmod(z + 4), 1), "b5")
    b_out(4)
    forward((2, 6))
    audio_piece(1)
    ring(3)
    forward((3,))
    pick_rows(x, (0,), first=True)
    audio_piece(2)
    ring(4)
    forward((5, 4))
    audio_piece(3)

    @pl.loop(0, ENC // 256)
    def _(m):
        at = pl.ds(pl.multiple_of(m * 256, 256), 256)
        audio[at, :] = dot(acts[at, :], b_all[x])

    def audio_rows(xt, w):
        rows = [
            audio[pl.ds(pl.multiple_of((xt + X * zl) * EROWS, 32), EROWS), w * HALF : (w + 1) * HALF]
            for zl in range(2)
        ]
        return jnp.concatenate(rows, axis=0)

    for w, (step, side) in enumerate(sides):
        aud_send[0, w] = audio_rows(xmod(x + 2), w).astype(bf16)
        send(aud_send.at[0, w], aud_relay.at[w], ("aud1", w), side)
        aud_send[1, w] = audio_rows(xmod(x + step), 1 - w).astype(bf16)
        send(aud_send.at[1, w], aud_recv.at[1, w], ("aud2", w), side)

    def audio_relay():
        for w, (step, side) in enumerate(sides):
            arrived(aud_relay.at[w], "aud1", w)
            aud_send[2, w] = (audio_rows(xmod(x + step), w) + aud_relay[w].astype(f32)).astype(bf16)
            send(aud_send.at[2, w], aud_recv.at[0, w], ("aud3", w), side)

    def turn(first, last):
        @pl.loop(first, last)
        def _(i):
            zs = zmod(z + i)
            for j in range(2):
                a_t[:, pl.ds(pl.multiple_of(zs * LIVE + j * 128, 128), 128)] = a_all[
                    zs, j * 128 : (j + 1) * 128, :
                ].T

    pick_rows(x, (1,))
    ring(5)
    pick_rows(xmod(x - 1), (0, 1))
    ring(6)
    audio_relay()
    pick_rows(xmod(x + 1), (0, 1))
    turn(-2, 3)
    for k in range(Z):
        arrived(b_rows(xmod(x + 2), zmod(z - k)), "fr" if k < 4 else "fl", k)
    pick_rows(xmod(x + 2), (0, 1), last=True)

    for t in range(3):
        for j in range(2):
            if (t + 1, j) not in up_items:
                arrived(a_rows(zmod(z - t - 1), j), "up", t, j)
            if (t + 1, j) not in down_items:
                arrived(a_rows(zmod(z + t + 1), j), "down", t, j)
    arrived(a_rows(zmod(z + 4), 0), "up", 3, 0)
    arrived(a_rows(zmod(z + 4), 1), "down", 3, 1)
    turn(3, 6)

    aud_part[...] = jnp.zeros_like(aud_part)
    sums = []
    for w in range(2):
        arrived(aud_recv.at[0, w], "aud3", w)
        arrived(aud_recv.at[1, 1 - w], "aud2", 1 - w)
        sums.append(audio_rows(x, w) + aud_recv[0, w].astype(f32) + aud_recv[1, 1 - w].astype(f32))
    audio[0 : 2 * EROWS, :] = jnp.concatenate(sums, axis=1)
    for zl in range(2):
        for d in range(Y * C):
            at = zl * EROWS + d * AROWS
            aud_part[zl, d, 0:AROWS, :] = audio[at : at + AROWS, :]

    other = 1 - core

    for zl in range(2):
        for m in range(2):
            at = pl.ds(zl * ZROWS + m * (ZROWS // 2), ZROWS // 2)
            merger[at, :] = dot(a_t[at, :], picked_b[...])

        def merger_rows(d):
            return merger[pl.ds(pl.multiple_of(zl * ZROWS + d * ROWS, 16), ROWS), :]

        for yt in range(Y):
            core_send[zl, yt, 0:ROWS, :] = merger_rows(2 * yt + other)
            core_send[zl, yt, ROWS:, :] = aud_part[zl, 2 * yt + other]
        send(core_send.at[zl], core_recv.at[zl], ("core", zl), {"core": other})
        for yt in range(Y):
            own[zl, yt, 0:ROWS, :] = merger_rows(2 * yt + core)
            own[zl, yt, ROWS:, :] = aud_part[zl, 2 * yt + core]

    y_sides = ((1, {"y": ymod(y + 1)}), (-1, {"y": ymod(y + Y - 1)}))

    def y_part(zl, yt, w):
        cols = slice(w * HALF, (w + 1) * HALF)
        return own[zl, yt, :, cols] + core_recv[zl, yt, :, cols]

    for zl in range(2):
        arrived(core_recv.at[zl], "core", zl)
        for w, (step, side) in enumerate(y_sides):
            y_send[zl, 0, w] = y_part(zl, ymod(y + 2), w).astype(bf16)
            send(y_send.at[zl, 0, w], y_relay.at[zl, w], ("y1", zl, w), side)
        for w, (step, side) in enumerate(y_sides):
            y_send[zl, 1, w] = y_part(zl, ymod(y + Y + step), 1 - w).astype(bf16)
            send(y_send.at[zl, 1, w], y_recv.at[zl, 1, w], ("y2", zl, w), side)
    for zl in range(2):
        for w, (step, side) in enumerate(y_sides):
            arrived(y_relay.at[zl, w], "y1", zl, w)
            y_send[zl, 2, w] = (y_part(zl, ymod(y + Y + step), w) + y_relay[zl, w].astype(f32)).astype(bf16)
            send(y_send.at[zl, 2, w], y_recv.at[zl, 0, w], ("y3", zl, w), side)

    fin = [(sem("fin", k), sem("fin", k + 2)) for k in (0, 1)]
    fin_out = [(sem("fout", k), sem("fout", k + 2)) for k in (0, 1)]
    assert fin[1][0] - fin[0][0] == 2

    def last(zl):
        device = {"z": x + X * zl, "x": home_x}
        return [
            pltpu.make_async_remote_copy(
                src_ref=src.at[zl], dst_ref=dst.at[half], send_sem=ssem.at[fin_out[zl][i]],
                recv_sem=rsem.at[fin[0][i] + 2 * half], device_id=device, device_id_type=MESH,
            )
            for i, (src, dst) in enumerate(((fin_send, fin_recv), (fina_send, fina_recv)))
        ]

    for zl in range(2):
        sums = []
        for w in range(2):
            arrived(y_recv.at[zl, 0, w], "y3", zl, w)
            arrived(y_recv.at[zl, 1, 1 - w], "y2", zl, 1 - w)
            sums.append(y_part(zl, y, w) + y_recv[zl, 0, w].astype(f32) + y_recv[zl, 1, 1 - w].astype(f32))
        total = jnp.concatenate(sums, axis=1)
        fin_send[zl] = total[0:ROWS].astype(bf16)
        fina_send[zl] = total[ROWS : ROWS + KEEP]
        elsewhere = jnp.logical_or(x + X * zl != z, home_x != x)

        @pl.when(elsewhere)
        def _():
            for c in last(zl):
                c.start()

        @pl.when(jnp.logical_not(elsewhere))
        def _():
            fin_recv[half] = fin_send[zl]
            fina_recv[half] = fina_send[zl]

    for h in range(2):
        @pl.when(jnp.logical_or(2 * x + h != z, lax.rem(z, X) != x))
        def _():
            for i, buffer in enumerate((fin_recv, fina_recv)):
                pltpu.make_async_remote_copy(
                    src_ref=buffer.at[h], dst_ref=buffer.at[h], send_sem=ssem.at[fin_out[0][i]],
                    recv_sem=rsem.at[fin[h][i]], device_id={"core": other}, device_id_type=MESH,
                ).wait_recv()

    out_m[:, 0:WIDE] = fin_recv[0].astype(f32)
    out_m[:, WIDE:] = fin_recv[1].astype(f32)[:, 2 * WIDE - BLOCK :]
    out_a[:, 0:WIDE] = fina_recv[0, 0:AROWS, :]
    out_a[:, WIDE:] = fina_recv[1, 0:AROWS, 2 * WIDE - BLOCK :]

    for c in sent:
        c.wait_send()
    for zl in range(2):

        @pl.when(jnp.logical_or(x + X * zl != z, home_x != x))
        def _():
            for c in last(zl):
                c.wait_send()

    assert len(names) <= 192


def local(mel, conv_weight, conv_bias, video_hidden, video_count, video_places, audio_places, cotangent):
    vmem = pl.BlockSpec(memory_space=pltpu.VMEM)
    hbm = pl.BlockSpec(memory_space=pl.ANY)
    part = (PART, WIDE)
    merger, audio = pl.pallas_call(
        kernel,
        out_shape=(
            jax.ShapeDtypeStruct((ROWS, BLOCK), f32),
            jax.ShapeDtypeStruct((AROWS, BLOCK), f32),
        ),
        in_specs=[vmem, vmem, vmem, hbm, vmem, vmem, vmem, hbm],
        out_specs=(vmem, vmem),
        scratch_shapes=[
            pltpu.VMEM((8, 128), i32),
            pltpu.VMEM((X, 8, 128), i32),
            pltpu.VMEM((X, Z, 8, 128), i32),
            pltpu.VMEM((X, Z, FRAMES, MELS), bf16),
            pltpu.VMEM((X, Z * SPOTS, WIDE), bf16),
            pltpu.VMEM((X, SLOTS, RROWS), bf16),
            pltpu.VMEM((Z, LIVE, RROWS), bf16),
            pltpu.VMEM((RROWS, Z * LIVE), bf16),
            pltpu.VMEM((X * Z * FRAMES, 4 * MELS), bf16),
            pltpu.VMEM((ENC, 4 * MELS), bf16),
            pltpu.VMEM((128, ENC), bf16),
            pltpu.VMEM((Z * LIVE, 128), i32),
            pltpu.VMEM((Z * LIVE, WIDE), f32),
            pltpu.VMEM((Z * LIVE, WIDE), bf16),
            pltpu.VMEM((RROWS, WIDE), f32),
            pltpu.VMEM((ENC, Z * SPOTS), bf16),
            pltpu.VMEM((ENC, WIDE), f32),
            pltpu.VMEM((3, 2, 2 * EROWS, HALF), bf16),
            pltpu.VMEM((2, 2 * EROWS, HALF), bf16),
            pltpu.VMEM((2, 2, 2 * EROWS, HALF), bf16),
            pltpu.VMEM((2, Y * C, APAD, WIDE), f32),
            pltpu.VMEM((2, Y, *part), f32),
            pltpu.VMEM((2, Y, *part), f32),
            pltpu.VMEM((2, Y, *part), f32),
            pltpu.VMEM((2, 3, 2, PART, HALF), bf16),
            pltpu.VMEM((2, 2, PART, HALF), bf16),
            pltpu.VMEM((2, 2, 2, PART, HALF), bf16),
            pltpu.VMEM((2, ROWS, WIDE), bf16),
            pltpu.VMEM((2, ROWS, WIDE), bf16),
            pltpu.VMEM((2, KEEP, WIDE), f32),
            pltpu.VMEM((2, KEEP, WIDE), f32),
            pltpu.VMEM((2, SLOTS, ZROWS), bf16),
            pltpu.VMEM((SPOTS // 2, WIDE), bf16),
            pltpu.SemaphoreType.DMA((192,)),
            pltpu.SemaphoreType.DMA((192,)),
        ],
        compiler_params=pltpu.CompilerParams(
            collective_id=0, has_side_effects=True, vmem_limit_bytes=60 * 2**20
        ),
    )(
        mel[0], conv_weight, conv_bias[None], video_hidden[0],
        video_count, video_places, audio_places, cotangent[0],
    )
    return merger[None], audio[None]


def solution(mesh):
    whole = Mesh(mesh.devices.reshape(Z, X, Y, C), ("z", "x", "y", "core"))
    dp, ctx = ("y", "core"), ("z", "x")
    return jax.shard_map(
        local,
        mesh=whole,
        in_specs=(
            P(dp, ctx, None),
            P(),
            P(),
            P(dp, ctx, None),
            P(dp, ctx),
            P(dp, ctx),
            P(dp, ctx),
            P(dp, ctx, None),
        ),
        out_specs=(P(ctx, dp, None), P(ctx, dp, None)),
        check_vma=False,
    )
```

```python
import jax
import jax.numpy as jnp
from jax import lax
from jax.experimental import pallas as pl
from jax.experimental.pallas import tpu as pltpu
from jax.sharding import Mesh, PartitionSpec as P

Z, X, Y, C = 8, 4, 4, 2
MELS, ENC, HID, OUT = 128, 1280, 5120, 3584
FRAMES, SLOTS, SPOTS = 128, 128, 192
BLOCK = OUT // X
WIDE = 512
MAIN = 384
RROWS = HID // X
ROWS = HID // Z // (Y * C)
AROWS = ENC // Z // (Y * C)
APAD = 32
PART = ROWS + APAD
KEEP = 24
HALF = 256
EROWS = ENC // Z
ZROWS = HID // Z
LIVE = 256

bf16, f32, i32 = jnp.bfloat16, jnp.float32, jnp.int32
MESH = pl.DeviceIdType.MESH


def dot(a, b, dims=((1,), (0,))):
    return lax.dot_general(a, b, (dims, ((), ())), preferred_element_type=f32)


def iota(shape, dim):
    return lax.broadcasted_iota(i32, shape, dim)


def one_hot(mask):
    return jnp.where(mask, 1.0, 0.0).astype(bf16)


def kernel(
    mel, convw, bias, hidden, count, vplaces, aplaces, cot,
    out_m, out_a,
    ints, ints_x, ints_all, mel_all, b_all, a_raw, a_all, a_t, windows, conv_t, w_ext,
    spot, picked, picked_b, merger, acts, audio, aud_send, aud_relay, aud_recv, aud_part, own, core_send, core_recv,
    y_send, y_relay, y_recv, fin_send, fin_recv, fina_send, fina_recv, a_relay, b_relay, ssem, rsem,
):
    z, x = lax.axis_index("z"), lax.axis_index("x")
    y, core = lax.axis_index("y"), lax.axis_index("core")

    def zmod(v):
        return lax.rem(v + 2 * Z, Z)

    def xmod(v):
        return lax.rem(v + 2 * X, X)

    def ymod(v):
        return lax.rem(v + Y, Y)

    home_x = lax.div(z, 2)
    half = lax.rem(z, 2)

    b_all[x, :, MAIN:] = jnp.zeros((Z * SPOTS, WIDE - MAIN), bf16)

    barrier = pltpu.get_barrier_semaphore()
    peers = [{"z": zmod(z + k)} for k in range(1, Z)]
    peers += [{"x": xmod(x + k)} for k in range(1, X)]
    peers += [{"y": ymod(y + k)} for k in range(1, Y)]
    peers += [{"core": 1 - core}]
    for peer in peers:
        pl.semaphore_signal(barrier, inc=1, device_id=peer, device_id_type=MESH)
    for h in range(2):

        @pl.when(jnp.logical_or(2 * x + h != z, lax.rem(z, X) != x))
        def _():
            pl.semaphore_signal(
                barrier, inc=1, device_id={"z": 2 * x + h, "x": lax.rem(z, X)}, device_id_type=MESH
            )

    here = jnp.logical_and(home_x == x, lax.rem(z, X) == x)
    pl.semaphore_wait(barrier, len(peers) + 2 - jnp.where(here, 1, 0))

    sent = []
    names = {}

    def sem(*key):
        return names.setdefault(key, len(names))

    def copy(src, dst, key, device):
        i = sem(*key)
        return pltpu.make_async_remote_copy(
            src_ref=src, dst_ref=dst, send_sem=ssem.at[i], recv_sem=rsem.at[i],
            device_id=device, device_id_type=MESH,
        )

    def send(src, dst, key, device):
        c = copy(src, dst, key, device)
        c.start()
        sent.append(c)

    def arrived(dst, *key):
        copy(dst, dst, key, {"core": 1 - core}).wait_recv()

    main, rest = pl.ds(0, MAIN), pl.ds(MAIN, WIDE - MAIN)

    def main_cols(zt):
        return pl.ds(pl.multiple_of(lax.div(zt, 2) * BLOCK + lax.rem(zt, 2) * WIDE, 128), MAIN)

    def rest_cols(zt):
        return pl.ds(pl.multiple_of(lax.div(zt, 2) * BLOCK + MAIN, 128), WIDE - MAIN)

    def even(zt):
        return lax.rem(zt, 2) == 0

    maybe = []

    def send_wide(pieces, key, zt, device):
        send(*pieces[0], key, device)

        @pl.when(even(zt))
        def _():
            copy(*pieces[1], (*key, "rest"), device).start()

        maybe.append((zt, lambda: copy(*pieces[1], (*key, "rest"), device)))

    def arrived_wide(refs, zt, *key):
        arrived(refs[0], *key)

        @pl.when(even(zt))
        def _():
            arrived(refs[1], *key, "rest")

    def b_rows(xs, zs):
        return b_all.at[xs, pl.ds(pl.multiple_of(zs * SPOTS, 64), SPOTS)]

    def b_parts(zs, first=0, count=SPOTS):
        rows = pl.ds(pl.multiple_of(zs * SPOTS + first, 32), count)
        return b_all.at[x, rows, main], b_all.at[x, rows, rest]

    def cot_parts(zt, first=0, count=SPOTS):
        rows = pl.ds(first, count)
        return cot.at[rows, main_cols(zt)], cot.at[rows, rest_cols(zt)]

    relay_parts = b_relay.at[:, main], b_relay.at[:, rest]

    def a_cols(xt, w):
        return hidden.at[:, pl.ds(pl.multiple_of((xt + X * w) * ZROWS, 128), ZROWS)]

    def a_slot(xs, w):
        return a_raw.at[xs, :, pl.ds(w * ZROWS, ZROWS)]

    right, left = {"x": xmod(x + 1)}, {"x": xmod(x - 1)}
    sides = ((1, right), (-1, left))

    ints[0:1, :] = aplaces[...]
    ints[1:2, :] = vplaces[...]
    ints[2:3, :] = jnp.broadcast_to(count[...], (1, 128))
    ints[3:8, :] = jnp.zeros((5, 128), i32)
    ints_x[x] = ints[...]
    ints_all[x, z] = ints[...]
    mel_all[x, z] = mel[...]

    for k in range(1, Z):
        zt = zmod(z + k)
        send(ints, ints_all.at[x, z], ("iz", k), {"z": zt})
        send(mel, mel_all.at[x, z], ("mz", k), {"z": zt})
    for k in range(1, X):
        send(ints, ints_x.at[x], ("ix", k), {"x": xmod(x + k)})
    for w, (step, side) in enumerate(sides):
        send(a_cols(xmod(x + 2), w), a_relay.at[w], ("a2", w), side)
    for step, side in sides:
        for w in range(2):
            send(a_cols(xmod(x + step), w), a_slot(x, w), ("a", step, w), side)
    own_a = []
    for w in range(2):
        c = pltpu.make_async_copy(a_cols(x, w), a_slot(x, w), ssem.at[sem("own_a", w)])
        c.start()
        own_a.append(c)
    own_b = []
    for i, (src, dst) in enumerate(zip(cot_parts(z), b_parts(z))):
        c = pltpu.make_async_copy(src, dst, ssem.at[sem("own_b", i)])
        c.start()
        own_b.append(c)
    zt = zmod(z + 4)
    send_wide(list(zip(cot_parts(zt, 96, 96), relay_parts)), ("b4",), zt, {"z": zmod(z - 1)})
    for k in (1, 7, 2, 6, 3, 5):
        zt = zmod(z + k)
        send_wide(list(zip(cot_parts(zt), b_parts(z))), ("b", k), zt, {"z": zt})
    zt = zmod(z + 4)
    send_wide(list(zip(cot_parts(zt, 0, 96), b_parts(z, 0, 96))), ("b", 4), zt, {"z": zt})

    def b_out(k):
        block = b_rows(x, zmod(z - k))
        send(block, block, ("br", k), right)
        send(block, block, ("bl", k), left)


    def selection(held):
        row, col = iota((128, 256), 0), iota((128, 256), 1)
        return one_hot(jnp.where(row < held, row, row - held + 128) == col)

    up, down = {"z": zmod(z + 1)}, {"z": zmod(z - 1)}
    up_items = [(0, 0), (0, 1), (1, 0), (1, 1), (2, 0), (2, 1), (3, 0)]
    down_items = [(0, 0), (0, 1), (1, 0), (1, 1), (2, 0), (2, 1), (3, 1)]

    def pair(j):
        return lax.rem(lax.div(x, 2) + j, 2)

    def a_rows(zs, j):
        return a_all.at[zs, pl.ds(pl.multiple_of(pair(j) * 128, 128), 128)]

    def pack(j):
        p = pair(j)
        held = jnp.broadcast_to(ints_x[2 * p, 2:3, :][:, 0:1], (128, 256))
        both = jnp.concatenate([a_raw[2 * p], a_raw[2 * p + 1]], axis=0)
        a_all[z, pl.ds(pl.multiple_of(p * 128, 128), 128), :] = dot(selection(held), both).astype(bf16)

    def ring(n):
        for items, name, step, device in ((up_items, "up", -1, up), (down_items, "down", 1, down)):
            t, j = items[n]
            rows = a_rows(zmod(z + step * t), j)
            if t:
                arrived(rows, name, t - 1, j)
            send(rows, rows, (name, t, j), device)

    for w, (step, side) in enumerate(sides):
        arrived(a_relay.at[w], "a2", w)
        send(a_relay.at[w], a_slot(xmod(x - step), w), ("a3", w), side)
    for c in own_b:
        c.wait()
    b_out(0)

    b0 = bias[...]
    hi = b0.astype(bf16).astype(f32)
    mid = (b0 - hi).astype(bf16).astype(f32)
    low = b0 - hi - mid
    row = iota((128, ENC), 0)
    w_ext[...] = jnp.where(row == 0, hi, jnp.where(row == 1, mid, jnp.where(row == 2, low, 0.0))).astype(bf16)
    conv_t[:, 0 : 3 * MELS] = convw[...].T
    conv_t[:, 3 * MELS :] = w_ext[...].T

    for k in range(1, Z):
        arrived(ints_all.at[x, zmod(z - k)], "iz", k)
        arrived(mel_all.at[x, zmod(z - k)], "mz", k)
    def mel_half(xs, w):
        return mel_all.at[xs, pl.ds(w * (Z // 2), Z // 2)]

    for k in range(1, X):
        send(ints_all.at[x], ints_all.at[x], ("ixa", k), {"x": xmod(x + k)})
    for w in range(2):
        for step, side in sides:
            send(mel_half(x, w), mel_half(x, w), ("mxa", step, w), side)

    for c in own_a:
        c.wait()
    for k in range(1, X):
        arrived(ints_x.at[xmod(x - k)], "ix", k)
    for w, (step, side) in enumerate(sides):
        for v in range(2):
            arrived(a_slot(xmod(x - step), v), "a", step, v)
    pack(0)
    ring(0)
    for w in range(2):
        arrived(a_slot(xmod(x + 2), w), "a3", w)
    pack(1)
    ring(1)

    def forward(ks):
        for k in ks:
            zs = zmod(z - k)
            block = b_rows(xmod(x - 1), zs)
            arrived(block, "br", k)
            if k < 4:
                send(block, block, ("fr", k), right)
            block = b_rows(xmod(x + 1), zs)
            arrived(block, "bl", k)
            if k >= 4:
                send(block, block, ("fl", k), left)

    def audio_piece(h):
        wpos = []
        for zs in (2 * h, 2 * h + 1):
            base = (zs * X + x) * SPOTS
            here = iota((SPOTS, 128), 0) + base
            total = jnp.zeros((SPOTS, 4 * MELS), f32)

            def shard(xs, total):
                hot = jnp.concatenate(
                    [
                        one_hot(jnp.broadcast_to(ints_all[xs, zt, 0:1, :], (SPOTS, 128)) == here)
                        for zt in range(Z)
                    ],
                    axis=1,
                )
                at = pl.ds(pl.multiple_of(xs * (Z * FRAMES), FRAMES), Z * FRAMES)
                return total + dot(hot, windows[at, :])

            wpos.append(lax.fori_loop(0, X, shard, total).astype(bf16))
        wpos = jnp.concatenate(wpos, axis=0)

        @pl.loop(0, ENC // 256)
        def _(m):
            at = pl.ds(pl.multiple_of(m * 256, 256), 256)
            conv = dot(conv_t[at, :], wpos, ((1,), (1,)))
            act = (0.5 * conv * (1.0 + lax.erf(conv * 0.7071067811865476))).astype(bf16)
            acts[at, h * 2 * SPOTS : (h + 1) * 2 * SPOTS] = act

    def b_in(ks):
        for k in ks:
            arrived_wide(b_parts(zmod(z - k)), z, "b", k)
            b_out(k)

    for w, (step, side) in enumerate(sides):
        rows = mel_half(xmod(x - step), w)
        arrived(rows, "mxa", step, w)
        send(rows, rows, ("mxb", w), side)
    zt = zmod(z - 3)
    arrived_wide(relay_parts, zt, "b4")
    send_wide(list(zip(relay_parts, b_parts(zmod(z + 1), 96, 96))), ("b5",), zt, {"z": zt})
    for k in (1, 7):
        arrived_wide(b_parts(zmod(z - k)), z, "b", k)
        b_out(k)

    forward((0,))
    for k in range(1, X):
        arrived(ints_all.at[xmod(x - k)], "ixa", k)
    for w, (step, side) in enumerate(sides):
        arrived(mel_half(xmod(x - step), 1 - w), "mxa", step, 1 - w)
        arrived(mel_half(xmod(x + 2), w), "mxb", w)

    windows[:, 3 * MELS :] = jnp.ones((X * Z * FRAMES, 128), bf16)
    edge = iota((FRAMES, MELS), 0)

    @pl.loop(0, Z)
    def _(zs):
        for xs in range(X):
            own_frames = mel_all[xs, zs].astype(f32)
            zp = zs if xs else jnp.maximum(zs - 1, 0)
            zn = zs if xs < X - 1 else jnp.minimum(zs + 1, Z - 1)
            before = mel_all[(xs - 1) % X, zp].astype(f32)
            after = mel_all[(xs + 1) % X, zn].astype(f32)
            if xs == 0:
                before = jnp.where(jnp.broadcast_to(zs, before.shape) == 0, 0.0, before)
            if xs == X - 1:
                after = jnp.where(jnp.broadcast_to(zs, after.shape) == Z - 1, 0.0, after)
            before = jnp.where(edge == 0, pltpu.roll(before, 1, 0), pltpu.roll(own_frames, 1, 0))
            after = jnp.where(
                edge == FRAMES - 1, pltpu.roll(after, FRAMES - 1, 0), pltpu.roll(own_frames, FRAMES - 1, 0)
            )
            at = pl.ds(pl.multiple_of((xs * Z + zs) * FRAMES, FRAMES), FRAMES)
            windows[at, 0:MELS] = before.astype(bf16)
            windows[at, MELS : 2 * MELS] = own_frames.astype(bf16)
            windows[at, 2 * MELS : 3 * MELS] = after.astype(bf16)

    b_in((2, 6))

    @pl.loop(0, Z)
    def _(zs):
        for j in range(2):
            held = jnp.broadcast_to(ints_all[2 * j, zs, 2:3, :][:, 0:1], (128, 256))
            pick = selection(held)
            places = jnp.concatenate([ints_all[2 * j, zs, 1:2, :], ints_all[2 * j + 1, zs, 1:2, :]], axis=1)
            high = lax.shift_right_logical(places, 7)
            rest = jnp.bitwise_and(places, 127)
            high = jnp.broadcast_to(high.astype(f32), (128, 256)).astype(bf16)
            rest = jnp.broadcast_to(rest.astype(f32), (128, 256)).astype(bf16)
            value = 128.0 * dot(pick, high, ((1,), (1,))) + dot(pick, rest, ((1,), (1,)))
            spot[pl.ds(pl.multiple_of(zs * LIVE + j * 128, 128), 128), :] = value.astype(i32)

    lane = iota((256, 128), 1)

    def pick_rows(xs, parts, first=False, last=False):
        span = 4 * SPOTS
        blocks = pl.ds(parts[0] * span, len(parts) * span)

        @pl.loop(0, Z)
        def _(q):
            at = pl.ds(pl.multiple_of(q * LIVE, LIVE), LIVE)
            spots = spot[at, :]
            tiles = []
            for part in parts:
                for t in range(span // 128):
                    ends = []
                    for s in (2 * t, 2 * t + 1):
                        ends.append((4 * part + s // 3) * X * SPOTS + (s % 3) * 64)
                    there = jnp.where(lane < 64, lane + ends[0], lane - 64 + ends[1]) + xs * SPOTS
                    tiles.append(one_hot(spots == there))
            got = dot(jnp.concatenate(tiles, axis=1), b_all[xs, blocks, :])
            if last:
                picked_b[at, :] = (picked[at, :] + got).astype(bf16)
            elif first:
                picked[at, :] = got
            else:
                picked[at, :] += got

    ring(2)
    b_in((3, 5))
    forward((1, 7))
    audio_piece(0)
    arrived_wide(b_parts(zmod(z + 4), 0, 96), z, "b", 4)
    arrived_wide(b_parts(zmod(z + 4), 96, 96), z, "b5")
    b_out(4)
    forward((2, 6))
    ring(3)
    audio_piece(1)
    forward((3,))
    pick_rows(x, (0,), first=True)
    audio_piece(2)
    ring(4)
    forward((5, 4))
    audio_piece(3)

    @pl.loop(0, ENC // 256)
    def _(m):
        at = pl.ds(pl.multiple_of(m * 256, 256), 256)
        audio[at, :] = dot(acts[at, :], b_all[x])

    def audio_rows(xt, w):
        rows = [
            audio[pl.ds(pl.multiple_of((xt + X * zl) * EROWS, 32), EROWS), w * HALF : (w + 1) * HALF]
            for zl in range(2)
        ]
        return jnp.concatenate(rows, axis=0)

    for w, (step, side) in enumerate(sides):
        aud_send[0, w] = audio_rows(xmod(x + 2), w).astype(bf16)
        send(aud_send.at[0, w], aud_relay.at[w], ("aud1", w), side)
        aud_send[1, w] = audio_rows(xmod(x + step), 1 - w).astype(bf16)
        send(aud_send.at[1, w], aud_recv.at[1, w], ("aud2", w), side)

    def audio_relay():
        for w, (step, side) in enumerate(sides):
            arrived(aud_relay.at[w], "aud1", w)
            aud_send[2, w] = (audio_rows(xmod(x + step), w) + aud_relay[w].astype(f32)).astype(bf16)
            send(aud_send.at[2, w], aud_recv.at[0, w], ("aud3", w), side)

    def turn(first, last):
        @pl.loop(first, last)
        def _(i):
            zs = zmod(z + i)
            for j in range(2):
                a_t[:, pl.ds(pl.multiple_of(zs * LIVE + j * 128, 128), 128)] = a_all[
                    zs, j * 128 : (j + 1) * 128, :
                ].T

    pick_rows(x, (1,))
    ring(5)
    pick_rows(xmod(x - 1), (0, 1))
    ring(6)
    audio_relay()
    pick_rows(xmod(x + 1), (0, 1))
    turn(-2, 3)
    aud_part[...] = jnp.zeros_like(aud_part)
    sums = []
    for w in range(2):
        arrived(aud_recv.at[0, w], "aud3", w)
        arrived(aud_recv.at[1, 1 - w], "aud2", 1 - w)
        sums.append(audio_rows(x, w) + aud_recv[0, w].astype(f32) + aud_recv[1, 1 - w].astype(f32))
    audio[0 : 2 * EROWS, :] = jnp.concatenate(sums, axis=1)
    for zl in range(2):
        for d in range(Y * C):
            at = zl * EROWS + d * AROWS
            aud_part[zl, d, 0:AROWS, :] = audio[at : at + AROWS, :]

    for k in range(Z):
        arrived(b_rows(xmod(x + 2), zmod(z - k)), "fr" if k < 4 else "fl", k)
    pick_rows(xmod(x + 2), (0, 1), last=True)

    for t in range(3):
        for j in range(2):
            if (t + 1, j) not in up_items:
                arrived(a_rows(zmod(z - t - 1), j), "up", t, j)
            if (t + 1, j) not in down_items:
                arrived(a_rows(zmod(z + t + 1), j), "down", t, j)
    arrived(a_rows(zmod(z + 4), 0), "up", 3, 0)
    arrived(a_rows(zmod(z + 4), 1), "down", 3, 1)
    turn(3, 6)

    other = 1 - core

    for zl in range(2):
        for m in range(2):
            at = pl.ds(zl * ZROWS + m * (ZROWS // 2), ZROWS // 2)
            merger[at, :] = dot(a_t[at, :], picked_b[...])

        def merger_rows(d):
            return merger[pl.ds(pl.multiple_of(zl * ZROWS + d * ROWS, 16), ROWS), :]

        for yt in range(Y):
            core_send[zl, yt, 0:ROWS, :] = merger_rows(2 * yt + other)
            core_send[zl, yt, ROWS:, :] = aud_part[zl, 2 * yt + other]
        send(core_send.at[zl], core_recv.at[zl], ("core", zl), {"core": other})
        for yt in range(Y):
            own[zl, yt, 0:ROWS, :] = merger_rows(2 * yt + core)
            own[zl, yt, ROWS:, :] = aud_part[zl, 2 * yt + core]

    y_sides = ((1, {"y": ymod(y + 1)}), (-1, {"y": ymod(y + Y - 1)}))

    def y_part(zl, yt, w):
        cols = slice(w * HALF, (w + 1) * HALF)
        return own[zl, yt, :, cols] + core_recv[zl, yt, :, cols]

    for zl in range(2):
        arrived(core_recv.at[zl], "core", zl)
        for w, (step, side) in enumerate(y_sides):
            y_send[zl, 0, w] = y_part(zl, ymod(y + 2), w).astype(bf16)
            send(y_send.at[zl, 0, w], y_relay.at[zl, w], ("y1", zl, w), side)
        for w, (step, side) in enumerate(y_sides):
            y_send[zl, 1, w] = y_part(zl, ymod(y + Y + step), 1 - w).astype(bf16)
            send(y_send.at[zl, 1, w], y_recv.at[zl, 1, w], ("y2", zl, w), side)
    for zl in range(2):
        for w, (step, side) in enumerate(y_sides):
            arrived(y_relay.at[zl, w], "y1", zl, w)
            y_send[zl, 2, w] = (y_part(zl, ymod(y + Y + step), w) + y_relay[zl, w].astype(f32)).astype(bf16)
            send(y_send.at[zl, 2, w], y_recv.at[zl, 0, w], ("y3", zl, w), side)

    fin = [(sem("fin", k), sem("fin", k + 2)) for k in (0, 1)]
    fin_out = [(sem("fout", k), sem("fout", k + 2)) for k in (0, 1)]
    assert fin[1][0] - fin[0][0] == 2

    def last(zl):
        device = {"z": x + X * zl, "x": home_x}
        return [
            pltpu.make_async_remote_copy(
                src_ref=src.at[zl], dst_ref=dst.at[half], send_sem=ssem.at[fin_out[zl][i]],
                recv_sem=rsem.at[fin[0][i] + 2 * half], device_id=device, device_id_type=MESH,
            )
            for i, (src, dst) in enumerate(((fin_send, fin_recv), (fina_send, fina_recv)))
        ]

    for zl in range(2):
        sums = []
        for w in range(2):
            arrived(y_recv.at[zl, 0, w], "y3", zl, w)
            arrived(y_recv.at[zl, 1, 1 - w], "y2", zl, 1 - w)
            sums.append(y_part(zl, y, w) + y_recv[zl, 0, w].astype(f32) + y_recv[zl, 1, 1 - w].astype(f32))
        total = jnp.concatenate(sums, axis=1)
        fin_send[zl] = total[0:ROWS].astype(bf16)
        fina_send[zl] = total[ROWS : ROWS + KEEP]
        elsewhere = jnp.logical_or(x + X * zl != z, home_x != x)

        @pl.when(elsewhere)
        def _():
            for c in last(zl):
                c.start()

        @pl.when(jnp.logical_not(elsewhere))
        def _():
            fin_recv[half] = fin_send[zl]
            fina_recv[half] = fina_send[zl]

    for h in range(2):
        @pl.when(jnp.logical_or(2 * x + h != z, lax.rem(z, X) != x))
        def _():
            for i, buffer in enumerate((fin_recv, fina_recv)):
                pltpu.make_async_remote_copy(
                    src_ref=buffer.at[h], dst_ref=buffer.at[h], send_sem=ssem.at[fin_out[0][i]],
                    recv_sem=rsem.at[fin[h][i]], device_id={"core": other}, device_id_type=MESH,
                ).wait_recv()

    out_m[:, 0:WIDE] = fin_recv[0].astype(f32)
    out_m[:, WIDE:] = fin_recv[1].astype(f32)[:, 0:MAIN]
    out_a[:, 0:WIDE] = fina_recv[0, 0:AROWS, :]
    out_a[:, WIDE:] = fina_recv[1, 0:AROWS, 0:MAIN]

    for c in sent:
        c.wait_send()
    for zt, again in maybe:

        @pl.when(even(zt))
        def _():
            again().wait_send()

    for zl in range(2):

        @pl.when(jnp.logical_or(x + X * zl != z, home_x != x))
        def _():
            for c in last(zl):
                c.wait_send()

    assert len(names) <= 192


def local(mel, conv_weight, conv_bias, video_hidden, video_count, video_places, audio_places, cotangent):
    vmem = pl.BlockSpec(memory_space=pltpu.VMEM)
    hbm = pl.BlockSpec(memory_space=pl.ANY)
    part = (PART, WIDE)
    merger, audio = pl.pallas_call(
        kernel,
        out_shape=(
            jax.ShapeDtypeStruct((ROWS, BLOCK), f32),
            jax.ShapeDtypeStruct((AROWS, BLOCK), f32),
        ),
        in_specs=[vmem, vmem, vmem, hbm, vmem, vmem, vmem, hbm],
        out_specs=(vmem, vmem),
        scratch_shapes=[
            pltpu.VMEM((8, 128), i32),
            pltpu.VMEM((X, 8, 128), i32),
            pltpu.VMEM((X, Z, 8, 128), i32),
            pltpu.VMEM((X, Z, FRAMES, MELS), bf16),
            pltpu.VMEM((X, Z * SPOTS, WIDE), bf16),
            pltpu.VMEM((X, SLOTS, RROWS), bf16),
            pltpu.VMEM((Z, LIVE, RROWS), bf16),
            pltpu.VMEM((RROWS, Z * LIVE), bf16),
            pltpu.VMEM((X * Z * FRAMES, 4 * MELS), bf16),
            pltpu.VMEM((ENC, 4 * MELS), bf16),
            pltpu.VMEM((128, ENC), bf16),
            pltpu.VMEM((Z * LIVE, 128), i32),
            pltpu.VMEM((Z * LIVE, WIDE), f32),
            pltpu.VMEM((Z * LIVE, WIDE), bf16),
            pltpu.VMEM((RROWS, WIDE), f32),
            pltpu.VMEM((ENC, Z * SPOTS), bf16),
            pltpu.VMEM((ENC, WIDE), f32),
            pltpu.VMEM((3, 2, 2 * EROWS, HALF), bf16),
            pltpu.VMEM((2, 2 * EROWS, HALF), bf16),
            pltpu.VMEM((2, 2, 2 * EROWS, HALF), bf16),
            pltpu.VMEM((2, Y * C, APAD, WIDE), f32),
            pltpu.VMEM((2, Y, *part), f32),
            pltpu.VMEM((2, Y, *part), f32),
            pltpu.VMEM((2, Y, *part), f32),
            pltpu.VMEM((2, 3, 2, PART, HALF), bf16),
            pltpu.VMEM((2, 2, PART, HALF), bf16),
            pltpu.VMEM((2, 2, 2, PART, HALF), bf16),
            pltpu.VMEM((2, ROWS, WIDE), bf16),
            pltpu.VMEM((2, ROWS, WIDE), bf16),
            pltpu.VMEM((2, KEEP, WIDE), f32),
            pltpu.VMEM((2, KEEP, WIDE), f32),
            pltpu.VMEM((2, SLOTS, ZROWS), bf16),
            pltpu.VMEM((SPOTS // 2, WIDE), bf16),
            pltpu.SemaphoreType.DMA((192,)),
            pltpu.SemaphoreType.DMA((192,)),
        ],
        compiler_params=pltpu.CompilerParams(
            collective_id=0, has_side_effects=True, vmem_limit_bytes=60 * 2**20
        ),
    )(
        mel[0], conv_weight, conv_bias[None], video_hidden[0],
        video_count, video_places, audio_places, cotangent[0],
    )
    return merger[None], audio[None]


def solution(mesh):
    whole = Mesh(mesh.devices.reshape(Z, X, Y, C), ("z", "x", "y", "core"))
    dp, ctx = ("y", "core"), ("z", "x")
    return jax.shard_map(
        local,
        mesh=whole,
        in_specs=(
            P(dp, ctx, None),
            P(),
            P(),
            P(dp, ctx, None),
            P(dp, ctx),
            P(dp, ctx),
            P(dp, ctx),
            P(dp, ctx, None),
        ),
        out_specs=(P(ctx, dp, None), P(ctx, dp, None)),
        check_vma=False,
    )
```
